32 devices in a mesh: row: 4 (over y, x), col: 8 (over z, core).
Axes of the slice: x: 2, y: 2, z: 4, core: 2. Of those that a mesh axis runs over, the one named last changes fastest.
Arguments:
- tiles: bfloat16 [4, 8, 32, 128, 128], P('row', 'col'), may hold values from -0.5 to 0.5
- tile_slots: int32 [4, 8, 32], P('row', 'col'), may hold values from 0 to 191, as said below
- tile_counts: int32 [4, 8], P('row', 'col'), may hold values from 8 to 32, as said below
- user_degree: int32 [8192], P('row'), may hold values from 1 to 64
- item_degree: int32 [12288], P('col'), may hold values from 1 to 64
- start_panel: float32 [64, 12288], P(None, ('col', 'row')), may hold values from -6 to 6
Outputs:
- left_panel: float32 [64, 8192], P(None, ('row', 'col'))
- right_panel: float32 [64, 12288], P(None, ('col', 'row'))
- left_factors: float32 [3, 64, 64], replicated
- right_factors: float32 [3, 64, 64], replicated
The draws below stay inside these ranges and needn't reach their ends.
Inputs may be any that keep to these rules, and one draw needn't show every extreme that they name: `tile_slots`: within one grid cell the 32 slot numbers are distinct; slot s is local tile row s // 12 and local tile column s % 12; entries from position tile_counts on are padding. `tile_counts`: some grid cell holds 32 live tiles.
All inputs are finite; a program needn't handle non-finite values.
Results may differ from the reference program's by a relative error of at most 0.0005.
Values sent between devices are 32-bit elements; how exact they have to be, the bound alone decides.
A program may use at most 64 MiB of HBM per device.

```python
import math
import jax
import jax.numpy as jnp
from jax import lax

BLOCK = 64
TILE = 128
STEPS = 3
RB_DEV = 16
CB_DEV = 12
MAXT = 32
GRID_R = 4
GRID_C = 8
USERS = 8192
ITEMS = 12288


def draw_tile_slots(key, part):
    cell_keys = jax.random.split(jax.random.fold_in(key, 3), GRID_R * GRID_C)

    def one_cell(cell_key):
        return jax.random.permutation(cell_key, RB_DEV * CB_DEV)[:MAXT]
    slot_table = jax.vmap(one_cell)(cell_keys).astype(jnp.int32)
    return slot_table.reshape(GRID_R, GRID_C, MAXT)


def draw_tile_counts(key, part):
    base_key = jax.random.fold_in(key, 5)
    counts = jax.random.randint(base_key, (GRID_R * GRID_C,), MAXT // 4, MAXT // 2 + 1)
    chosen_cell = jax.random.randint(jax.random.fold_in(key, 7), (), 0, GRID_R * GRID_C)
    counts = jnp.where(jnp.arange(GRID_R * GRID_C) == chosen_cell, MAXT, counts)
    return counts.astype(jnp.int32).reshape(GRID_R, GRID_C)


def degree_law(key, length):
    positions = jnp.arange(length, dtype=jnp.int32)
    limits = 8 + 57 * positions // length
    return (jax.random.randint(key, (length,), 0, limits) + 1).astype(jnp.int32)


def draw_user_degree(key, part):
    return degree_law(jax.random.fold_in(key, 11), USERS)


def draw_item_degree(key, part):
    return degree_law(jax.random.fold_in(key, 13), ITEMS)


def block_scale(key, dims, shards, least, largest):
    factor_of = 1.0
    for axis_at, blocks in shards:
        heights = jax.random.uniform(jax.random.fold_in(jax.random.fold_in(key, 6), axis_at), (blocks,), jnp.float32, least / len(shards), largest / len(shards))
        factor_of = factor_of * jnp.repeat(jnp.exp(heights), dims[axis_at] // blocks).reshape((-1,) + (1,) * (len(dims) - 1 - axis_at))
    return factor_of


def gaussian(rng, dims, scale, most, shards=(), kind=jnp.bfloat16):
    loudness = block_scale(rng, dims, shards, -0.22, 0.18) if shards else 1.0
    drawn = jax.random.normal(rng, dims, jnp.float32) * scale * loudness
    return jnp.minimum(jnp.maximum(drawn, -most), most).astype(kind)


def setup_inputs(seed: int = 0) -> dict:
    keys = jax.random.split(jax.random.key(seed), 7)
    tiles = gaussian(keys[0], (GRID_R, GRID_C, MAXT, TILE, TILE), 0.08, 0.5, ((0, 4), (1, 8)))
    tile_slots = draw_tile_slots(jax.random.fold_in(keys[6], 71), 0)
    tile_counts = draw_tile_counts(jax.random.fold_in(keys[6], 71), 0)
    user_degree = draw_user_degree(jax.random.fold_in(keys[6], 71), 0)
    item_degree = draw_item_degree(jax.random.fold_in(keys[6], 71), 0)
    start_panel = gaussian(keys[5], (BLOCK, ITEMS), 1.0, 6.0, ((1, 32),), jnp.float32)
    return {"tiles": tiles, "tile_slots": tile_slots, "tile_counts": tile_counts, "user_degree": user_degree, "item_degree": item_degree, "start_panel": start_panel}


HIGH = lax.Precision.HIGHEST

def orthonormal(vectors):
    gram_matrix = jnp.einsum('bn,cn->bc', vectors, vectors, precision=HIGH)
    factor = jnp.linalg.cholesky(gram_matrix)
    return (factor, lax.linalg.triangular_solve(factor, vectors, left_side=True, lower=True))

def grid_tables(tiles, tile_slots, tile_counts):
    grid_tiles = tiles.reshape(GRID_R, GRID_C * MAXT, TILE, TILE)
    grid_slots = tile_slots.reshape(GRID_R, GRID_C * MAXT).astype(jnp.int32)
    counts_rows = jnp.repeat(tile_counts.astype(jnp.int32), MAXT, axis=1)
    positions = jnp.arange(GRID_C * MAXT, dtype=jnp.int32)
    return (grid_tiles, grid_slots, counts_rows, positions)

def forward_product(tiles, tile_slots, tile_counts, vectors):
    grid_tiles, grid_slots, counts_rows, positions = grid_tables(tiles, tile_slots, tile_counts)
    column_owner = positions // MAXT
    panel_blocks = vectors.reshape(BLOCK, GRID_C * CB_DEV, TILE)

    def visit(grid_row, summed):
        grid_row = jnp.asarray(grid_row).astype(jnp.int32)
        tile_rows = lax.dynamic_index_in_dim(grid_tiles, grid_row, 0, keepdims=False).astype(jnp.float32)
        slot_row = lax.dynamic_index_in_dim(grid_slots, grid_row, 0, keepdims=False)
        count_row = lax.dynamic_index_in_dim(counts_rows, grid_row, 0, keepdims=False)
        live_mask = (positions % MAXT < count_row).astype(jnp.float32)
        item_index = (column_owner * CB_DEV + slot_row % CB_DEV).astype(jnp.int32)
        user_index = (grid_row * RB_DEV + slot_row // CB_DEV).astype(jnp.int32)
        chosen = panel_blocks[:, item_index, :].astype(jnp.float32)
        partial_value = jnp.einsum('mrc,bmc->bmr', tile_rows, chosen, precision=HIGH) * live_mask[None, :, None]
        return summed.at[:, user_index, :].add(partial_value)
    summed = lax.fori_loop(0, GRID_R, visit, jnp.zeros((BLOCK, GRID_R * RB_DEV, TILE), jnp.float32))
    return summed.reshape(BLOCK, USERS)

def backward_product(tiles, tile_slots, tile_counts, vectors):
    grid_tiles, grid_slots, counts_rows, positions = grid_tables(tiles, tile_slots, tile_counts)
    column_owner = positions // MAXT
    panel_blocks = vectors.reshape(BLOCK, GRID_R * RB_DEV, TILE)

    def visit(grid_row, summed):
        grid_row = jnp.asarray(grid_row).astype(jnp.int32)
        tile_rows = lax.dynamic_index_in_dim(grid_tiles, grid_row, 0, keepdims=False).astype(jnp.float32)
        slot_row = lax.dynamic_index_in_dim(grid_slots, grid_row, 0, keepdims=False)
        count_row = lax.dynamic_index_in_dim(counts_rows, grid_row, 0, keepdims=False)
        live_mask = (positions % MAXT < count_row).astype(jnp.float32)
        item_index = (column_owner * CB_DEV + slot_row % CB_DEV).astype(jnp.int32)
        user_index = (grid_row * RB_DEV + slot_row // CB_DEV).astype(jnp.int32)
        chosen = panel_blocks[:, user_index, :].astype(jnp.float32)
        partial_value = jnp.einsum('mrc,bmr->bmc', tile_rows, chosen, precision=HIGH) * live_mask[None, :, None]
        return summed.at[:, item_index, :].add(partial_value)
    summed = lax.fori_loop(0, GRID_R, visit, jnp.zeros((BLOCK, GRID_C * CB_DEV, TILE), jnp.float32))
    return summed.reshape(BLOCK, ITEMS)

def reference(tiles, tile_slots, tile_counts, user_degree, item_degree, start_panel):
    user_scale = lax.rsqrt(user_degree.astype(jnp.float32))
    item_scale = lax.rsqrt(item_degree.astype(jnp.float32))
    start_factor, item_basis = orthonormal(start_panel)
    user_basis = start_panel[:, :0]
    item_factor = start_factor
    user_list = []
    item_list = []
    for iteration in range(STEPS):
        scaled = item_basis * item_scale[None, :]
        forward = forward_product(tiles, tile_slots, tile_counts, scaled) * user_scale[None, :]
        if iteration > 0:
            forward = forward - jnp.dot(item_factor.T, user_basis, precision=HIGH)
        user_factor, user_basis = orthonormal(forward)
        scaled = user_basis * user_scale[None, :]
        backward = backward_product(tiles, tile_slots, tile_counts, scaled) * item_scale[None, :]
        backward = backward - jnp.dot(user_factor.T, item_basis, precision=HIGH)
        item_factor, item_basis = orthonormal(backward)
        user_list.append(user_factor)
        item_list.append(item_factor)
    return (math.sqrt(USERS) * user_basis, math.sqrt(ITEMS) * item_basis, jnp.stack(user_list), jnp.stack(item_list))
```

```python
import functools
import math

import jax
import jax.numpy as jnp
from jax import lax
from jax.experimental import pallas as pl
from jax.experimental.pallas import tpu as pltpu
from jax.sharding import PartitionSpec as P

STEPS = 3


HIGH = lax.Precision.HIGHEST


def gram_of(vectors):
    return jnp.einsum("bn,cn->bc", vectors, vectors, precision=HIGH)


def solve_lower(factor, vectors):
    return lax.linalg.triangular_solve(factor, vectors, left_side=True, lower=True)


def per_device_arrays(tiles, tile_slots, tile_counts, user_degree, item_degree, start_panel):
    tile_stack = tiles[0, 0].astype(jnp.float32)
    slot_list = tile_slots[0, 0]
    tile_total = tile_counts[0, 0]
    slot_count = tile_stack.shape[0]
    tile_width = tile_stack.shape[1]
    row_blocks = user_degree.shape[0] // tile_width
    col_blocks = item_degree.shape[0] // tile_width
    block_width = start_panel.shape[0]
    live_mask = jnp.arange(slot_count) < tile_total
    local_rows = slot_list // col_blocks
    local_cols = slot_list % col_blocks
    row_select = (
        (local_rows[:, None] == jnp.arange(row_blocks)[None, :]) & live_mask[:, None]
    ).astype(jnp.float32)
    col_select = (
        (local_cols[:, None] == jnp.arange(col_blocks)[None, :]) & live_mask[:, None]
    ).astype(jnp.float32)
    user_scale = lax.rsqrt(user_degree.astype(jnp.float32))
    item_scale = lax.rsqrt(item_degree.astype(jnp.float32))
    user_group = row_blocks * tile_width // lax.axis_size("col")
    item_group = col_blocks * tile_width // lax.axis_size("row")
    user_offset = lax.axis_index("col") * user_group
    item_offset = lax.axis_index("row") * item_group
    user_scale_own = lax.dynamic_slice_in_dim(user_scale, user_offset, user_group)
    item_scale_own = lax.dynamic_slice_in_dim(item_scale, item_offset, item_group)
    start_total = lax.psum(gram_of(start_panel), ("row", "col"))
    start_factor = jnp.linalg.cholesky(start_total)
    item_basis = solve_lower(start_factor, start_panel)
    user_basis = start_panel[:, :0]
    item_factor = start_factor
    user_list = []
    item_list = []
    for iteration in range(STEPS):
        scaled = item_basis * item_scale_own[None, :]
        item_full = lax.all_gather(scaled, "row", axis=1, tiled=True)
        forward_panel_blocks = item_full.reshape(block_width, col_blocks, tile_width)
        forward_chosen = jnp.take(forward_panel_blocks, local_cols, axis=1)
        forward_partial_value = jnp.einsum(
            "mrc,bmc->bmr", tile_stack, forward_chosen, precision=HIGH
        )
        forward_summed = jnp.einsum(
            "bmr,mk->bkr", forward_partial_value, row_select, precision=HIGH
        )
        forward = (
            lax.psum_scatter(
                forward_summed.reshape(block_width, row_blocks * tile_width),
                "col",
                scatter_dimension=1,
                tiled=True,
            )
            * user_scale_own[None, :]
        )
        if iteration > 0:
            forward = forward - jnp.dot(item_factor.T, user_basis, precision=HIGH)
        user_factor = jnp.linalg.cholesky(lax.psum(gram_of(forward), ("row", "col")))
        user_basis = solve_lower(user_factor, forward)
        scaled = user_basis * user_scale_own[None, :]
        user_full = lax.all_gather(scaled, "col", axis=1, tiled=True)
        panel_blocks = user_full.reshape(block_width, row_blocks, tile_width)
        chosen = jnp.take(panel_blocks, local_rows, axis=1)
        partial_value = jnp.einsum("mrc,bmr->bmc", tile_stack, chosen, precision=HIGH)
        summed = jnp.einsum("bmc,mk->bkc", partial_value, col_select, precision=HIGH)
        backward = (
            lax.psum_scatter(
                summed.reshape(block_width, col_blocks * tile_width),
                "row",
                scatter_dimension=1,
                tiled=True,
            )
            * item_scale_own[None, :]
        )
        backward = backward - jnp.dot(user_factor.T, item_basis, precision=HIGH)
        item_factor = jnp.linalg.cholesky(lax.psum(gram_of(backward), ("row", "col")))
        item_basis = solve_lower(item_factor, backward)
        user_list.append(user_factor)
        item_list.append(item_factor)
    user_total = row_blocks * tile_width * lax.axis_size("row")
    item_total = col_blocks * tile_width * lax.axis_size("col")
    return (
        math.sqrt(user_total) * user_basis,
        math.sqrt(item_total) * item_basis,
        jnp.stack(user_list),
        jnp.stack(item_list),
    )


MESH = pl.DeviceIdType.MESH
NT = (((1,), (1,)), ((), ()))
NN = (((1,), (0,)), ((), ()))


def dot_high(a, b, dims=NN):
    return lax.dot_general(
        a, b, dims, precision=HIGH, preferred_element_type=jnp.float32
    )


def factor_and_inverse(gram):
    n = gram.shape[0]
    blocks = n // 8
    eye = (
        lax.broadcasted_iota(jnp.int32, (n, n), 0)
        == lax.broadcasted_iota(jnp.int32, (n, n), 1)
    ).astype(jnp.float32)
    work = jnp.concatenate([gram, eye], axis=1)
    sub = lax.broadcasted_iota(jnp.int32, (8, 2 * n), 0)

    def block_step(b, parts):
        parts = list(parts)
        live = [None] + [
            (jnp.zeros((8, 2 * n), jnp.int32) + b < blocks - i).astype(jnp.float32)
            for i in range(1, blocks)
        ]
        for s in range(8):
            column = jnp.broadcast_to(parts[0][:, s : s + 1], (8, 2 * n))
            pivot = jnp.broadcast_to(column[s : s + 1, :], (8, 2 * n))
            scale = lax.rsqrt(pivot)
            row = jnp.broadcast_to(parts[0][s : s + 1, :], (8, 2 * n)) * scale
            for i in range(1, blocks):
                other = jnp.broadcast_to(parts[i][:, s : s + 1], (8, 2 * n))
                parts[i] = parts[i] - (other * live[i]) * (row * scale)
            below = parts[0] - (column * scale) * row
            parts[0] = jnp.where(sub > s, below, jnp.where(sub == s, row, parts[0]))
        parts = [pltpu.roll(p, 2 * n - 8, 1) for p in parts]
        return tuple(parts[1:] + parts[:1])

    parts = tuple(work[8 * i : 8 * i + 8] for i in range(blocks))
    parts = lax.fori_loop(0, blocks, block_step, parts)
    work = jnp.concatenate(parts, axis=0)
    upper = lax.broadcasted_iota(jnp.int32, (n, n), 0) <= lax.broadcasted_iota(
        jnp.int32, (n, n), 1
    )
    return jnp.where(upper, work[:, n:], 0.0), work[:, :n]


def kernel(
    n_row,
    n_col,
    row_blocks,
    col_blocks,
    index_ref,
    tiles_ref,
    user_degree_ref,
    item_degree_ref,
    start_ref,
    left_ref,
    right_ref,
    left_factor_ref,
    right_factor_ref,
    item_all,
    user_all,
    split,
    running,
    user_send,
    sibling_in,
    user_send2,
    user_in,
    item_send,
    item_in,
    item_raw,
    item_basis,
    user_basis,
    gram_own,
    gram_row,
    gram_sum,
    gram_col,
    s_gr,
    r_gr,
    s_gc,
    r_gc,
    s_ir,
    r_ir,
    s_uz,
    r_uz,
    s_us,
    r_us,
    s_sib,
    r_sib,
    s_z,
    r_z,
    s_row,
    r_row,
):
    row = lax.axis_index("row")
    col = lax.axis_index("col")
    n_z = n_col // 2
    core = lax.rem(col, 2)
    z = col // 2
    sibling = col + 1 - 2 * core
    slots = tiles_ref.shape[0]
    width = tiles_ref.shape[1]
    block = start_ref.shape[0]
    half = block // 2
    user_group = user_all.shape[2]
    item_group = item_all.shape[2]
    user_per = user_group // width
    item_per = item_group // width

    barrier = pltpu.get_barrier_semaphore()
    for d in range(1, n_row):
        pl.semaphore_signal(
            barrier, inc=1, device_id=(lax.rem(row + d, n_row), col), device_id_type=MESH
        )
    for d in range(1, n_col):
        pl.semaphore_signal(
            barrier, inc=1, device_id=(row, lax.rem(col + d, n_col)), device_id_type=MESH
        )
    pl.semaphore_wait(barrier, n_row + n_col - 2)

    def send(src, dst, s_sem, r_sem, target):
        copy = pltpu.make_async_remote_copy(
            src_ref=src,
            dst_ref=dst,
            send_sem=s_sem,
            recv_sem=r_sem,
            device_id=target,
            device_id_type=MESH,
        )
        copy.start()
        return copy

    user_scale = lax.rsqrt(user_degree_ref[pl.ds(col, 1), :].astype(jnp.float32))
    item_scale = lax.rsqrt(item_degree_ref[pl.ds(row, 1), :].astype(jnp.float32))

    def gram_start(raw, way):
        gram = dot_high(raw, raw, NT)
        gram_own[way] = jnp.concatenate([gram[:half], gram[half:]], axis=1)
        copies = []
        for d in range(1, n_row):
            copies.append(
                send(
                    gram_own.at[way],
                    gram_row.at[way, d],
                    s_gr.at[way, d],
                    r_gr.at[way, d],
                    (lax.rem(row + d, n_row), col),
                )
            )
        return copies

    def gram_middle(copies, way):
        gram_row[way, 0] = gram_own[way]
        for copy in copies:
            copy.wait_recv()
        total = gram_row[way, row]
        for i in range(1, n_row):
            total = total + gram_row[way, lax.rem(row - i + n_row, n_row)]
        gram_sum[way] = total
        out = []
        for d in range(1, n_col):
            out.append(
                send(
                    gram_sum.at[way],
                    gram_col.at[way, d],
                    s_gc.at[way, d],
                    r_gc.at[way, d],
                    (row, lax.rem(col + d, n_col)),
                )
            )
        return out

    def gram_end(copies, way):
        for copy in copies:
            copy.wait_recv()
        total = jnp.zeros((half, 2 * block), jnp.float32)
        gram_col[way, 0] = gram_sum[way]
        for j in range(n_col):
            total = total + gram_col[way, lax.rem(col - j + n_col, n_col)]
        gram = jnp.concatenate([total[:, :block], total[:, block:]], axis=0)
        return factor_and_inverse(gram)

    def put_split(first_block, values):
        for b in range(values.shape[1] // width):
            part = values[:, b * width : (b + 1) * width]
            high = part.astype(jnp.bfloat16)
            low = (part - high.astype(jnp.float32)).astype(jnp.bfloat16)
            split[first_block + b] = jnp.concatenate([high, low], axis=0)

    def products(base, dims):
        def one(t, total):
            tile = tiles_ref[index_ref[base + t]]
            vectors = split[index_ref[base + slots + t]]
            keep = index_ref[base + 2 * slots + t].astype(jnp.float32)
            both = lax.dot_general(
                vectors, tile, dims, preferred_element_type=jnp.float32
            )
            total = total * keep + (both[:block] + both[block:])
            running[t] = total
            return total

        lax.fori_loop(
            0, slots, one, jnp.zeros((block, width), jnp.float32), unroll=4
        )

    running[slots] = jnp.zeros((block, width), jnp.float32)
    forward_base = 0
    forward_last = 3 * slots
    backward_base = forward_last + row_blocks
    backward_last = backward_base + 3 * slots

    item_raw[...] = start_ref[...]
    user_basis[...] = jnp.zeros_like(user_basis)

    def step(k, carry):
        raw = item_raw[...]
        sent = gram_start(raw, 0)
        scaled = raw * item_scale
        item_all[row] = scaled
        moved = []
        for d in range(1, n_row):
            moved.append(
                send(
                    item_all.at[row],
                    item_all.at[row],
                    s_ir.at[d],
                    r_ir.at[d],
                    (lax.rem(row + d, n_row), col),
                )
            )
        put_split(row * item_per, scaled)
        sent2 = gram_middle(sent, 0)
        for d in range(1, n_row):
            moved[d - 1].wait_recv()
            source = lax.rem(row - d + n_row, n_row)
            put_split(source * item_per, item_all[source])
        products(forward_base, NT)
        pair = []
        for core_at in range(2):
            for z_at in range(n_z):
                for b in range(user_per):
                    user_send[core_at * n_z + z_at, :, b * width : (b + 1) * width] = (
                        running[
                            index_ref[
                                forward_last + (z_at * 2 + core_at) * user_per + b
                            ]
                        ]
                    )
        for d in list(range(1, n_z)) + [0]:
            target_z = lax.rem(z + d, n_z)
            pair.append(
                send(
                    user_send.at[(1 - core) * n_z + target_z],
                    sibling_in.at[target_z],
                    s_sib.at[d],
                    r_sib.at[d],
                    (row, sibling),
                )
            )
        across = []
        for d in range(1, n_z):
            target_z = lax.rem(z + d, n_z)
            pair[d - 1].wait_recv()
            user_send2[target_z] = (
                user_send[core * n_z + target_z] + sibling_in[target_z]
            )
            across.append(
                send(
                    user_send2.at[target_z],
                    user_in.at[z],
                    s_z.at[d],
                    r_z.at[d],
                    (row, target_z * 2 + core),
                )
            )
        pair[n_z - 1].wait_recv()
        summed = user_send[core * n_z + z] + sibling_in[z]
        factor_t, inverse = gram_end(sent2, 0)
        right_factor_ref[lax.rem(k + STEPS - 1, STEPS)] = factor_t.T
        item_basis[...] = dot_high(inverse, raw)
        correction = dot_high(factor_t, user_basis[...])
        for d in range(1, n_z):
            across[d - 1].wait_recv()
            summed = summed + user_in[lax.rem(z - d + n_z, n_z)]
        forward = dot_high(inverse, summed * user_scale) - correction
        for copy in sent + sent2 + moved + pair + across:
            copy.wait_send()

        sent = gram_start(forward, 1)
        scaled = forward * user_scale
        user_all[col] = scaled
        moved = []
        for d in range(1, n_z):
            moved.append(
                send(
                    user_all.at[col],
                    user_all.at[col],
                    s_uz.at[d],
                    r_uz.at[d],
                    (row, lax.rem(z + d, n_z) * 2 + core),
                )
            )
        passed = [
            send(
                user_all.at[col],
                user_all.at[col],
                s_us.at[0],
                r_us.at[0],
                (row, sibling),
            )
        ]
        put_split(col * user_per, scaled)
        sent2 = gram_middle(sent, 1)
        passed[0].wait_recv()
        put_split(sibling * user_per, user_all[sibling])
        for d in range(1, n_z):
            moved[d - 1].wait_recv()
            source = lax.rem(z - d + n_z, n_z) * 2 + core
            passed.append(
                send(
                    user_all.at[source],
                    user_all.at[source],
                    s_us.at[d],
                    r_us.at[d],
                    (row, sibling),
                )
            )
            put_split(source * user_per, user_all[source])
        for d in range(1, n_z):
            passed[d].wait_recv()
            source = lax.rem(z - d + n_z, n_z) * 2 + 1 - core
            put_split(source * user_per, user_all[source])
        products(backward_base, NN)
        for j in range(n_row):
            for b in range(item_per):
                item_send[j, :, b * width : (b + 1) * width] = running[
                    index_ref[backward_last + j * item_per + b]
                ]
        across = []
        for d in range(1, n_row):
            target = lax.rem(row + d, n_row)
            across.append(
                send(
                    item_send.at[target],
                    item_in.at[row],
                    s_row.at[d],
                    r_row.at[d],
                    (target, col),
                )
            )
        factor_t, inverse = gram_end(sent2, 1)
        left_factor_ref[k] = factor_t.T
        user_basis[...] = dot_high(inverse, forward)
        correction = dot_high(factor_t, item_basis[...])
        summed = item_send[row]
        for d in range(1, n_row):
            across[d - 1].wait_recv()
            summed = summed + item_in[lax.rem(row - d + n_row, n_row)]
        item_raw[...] = dot_high(inverse, summed * item_scale) - correction
        for copy in sent + sent2 + moved + passed + across:
            copy.wait_send()
        return carry

    lax.fori_loop(0, STEPS, step, 0)

    raw = item_raw[...]
    sent = gram_start(raw, 0)
    left_ref[...] = user_basis[...] * math.sqrt(row_blocks * width * n_row)
    sent2 = gram_middle(sent, 0)
    factor_t, inverse = gram_end(sent2, 0)
    right_factor_ref[STEPS - 1] = factor_t.T
    right_ref[...] = dot_high(inverse, raw) * math.sqrt(col_blocks * width * n_col)
    for copy in sent + sent2:
        copy.wait_send()


def order_tables(keys, partners, live, blocks):
    slots = keys.shape[0]
    at = jnp.arange(slots)
    rank_key = jnp.where(live, keys, blocks) * slots + at
    rank = jnp.sum((rank_key[None, :] < rank_key[:, None]).astype(jnp.int32), axis=1)
    placed = rank[None, :] == at[:, None]
    order = jnp.sum(jnp.where(placed, at[None, :], 0), axis=1)
    partner = jnp.sum(jnp.where(placed, partners[None, :], 0), axis=1)
    same = (keys[None, :] == keys[:, None]) & (live[None, :] & live[:, None])
    earlier = jnp.any(same & (at[None, :] < at[:, None]), axis=1)
    keep = jnp.sum(jnp.where(placed, earlier[None, :].astype(jnp.int32), 0), axis=1)
    mine = (keys[None, :] == jnp.arange(blocks)[:, None]) & live[None, :]
    last = jnp.max(jnp.where(mine, rank[None, :], -1), axis=1)
    last = jnp.where(last < 0, slots, last)
    return [order, partner, keep, last]


def per_device(tiles, tile_slots, tile_counts, user_degree, item_degree, start_panel):
    n_row, n_col = lax.axis_size("row"), lax.axis_size("col")
    slots, width = tiles.shape[2], tiles.shape[3]
    block = start_panel.shape[0]
    row_blocks = user_degree.shape[0] // width
    col_blocks = item_degree.shape[0] // width
    user_group = user_degree.shape[0] // n_col
    item_group = item_degree.shape[0] // n_row
    slot_list = tile_slots[0, 0]
    live = jnp.arange(slots) < tile_counts[0, 0]
    slot_list = jnp.where(live, slot_list, 0)
    local_rows, local_cols = slot_list // col_blocks, slot_list % col_blocks
    index = jnp.concatenate(
        order_tables(local_rows, local_cols, live, row_blocks)
        + order_tables(local_cols, local_rows, live, col_blocks)
    ).astype(jnp.int32)
    vmem = pl.BlockSpec(memory_space=pltpu.VMEM)
    f32 = jnp.float32
    dma = pltpu.SemaphoreType.DMA
    n_z = n_col // 2
    out = pl.pallas_call(
        functools.partial(kernel, n_row, n_col, row_blocks, col_blocks),
        out_shape=(
            jax.ShapeDtypeStruct((block, user_group), f32),
            jax.ShapeDtypeStruct((block, item_group), f32),
            jax.ShapeDtypeStruct((STEPS, block, block), f32),
            jax.ShapeDtypeStruct((STEPS, block, block), f32),
        ),
        in_specs=[pl.BlockSpec(memory_space=pltpu.SMEM)] + [vmem] * 4,
        out_specs=(vmem,) * 4,
        scratch_shapes=[
            pltpu.VMEM((n_row, block, item_group), f32),
            pltpu.VMEM((n_col, block, user_group), f32),
            pltpu.VMEM((max(row_blocks, col_blocks), 2 * block, width), jnp.bfloat16),
            pltpu.VMEM((slots + 1, block, width), f32),
            pltpu.VMEM((n_col, block, user_group), f32),
            pltpu.VMEM((n_z, block, user_group), f32),
            pltpu.VMEM((n_z, block, user_group), f32),
            pltpu.VMEM((n_z, block, user_group), f32),
            pltpu.VMEM((n_row, block, item_group), f32),
            pltpu.VMEM((n_row, block, item_group), f32),
            pltpu.VMEM((block, item_group), f32),
            pltpu.VMEM((block, item_group), f32),
            pltpu.VMEM((block, user_group), f32),
            pltpu.VMEM((2, block // 2, 2 * block), f32),
            pltpu.VMEM((2, n_row, block // 2, 2 * block), f32),
            pltpu.VMEM((2, block // 2, 2 * block), f32),
            pltpu.VMEM((2, n_col, block // 2, 2 * block), f32),
            dma((2, n_row)),
            dma((2, n_row)),
            dma((2, n_col)),
            dma((2, n_col)),
            dma((n_row,)),
            dma((n_row,)),
            dma((n_z,)),
            dma((n_z,)),
            dma((n_z,)),
            dma((n_z,)),
            dma((n_z,)),
            dma((n_z,)),
            dma((n_z,)),
            dma((n_z,)),
            dma((n_row,)),
            dma((n_row,)),
        ],
        compiler_params=pltpu.CompilerParams(
            collective_id=0, has_side_effects=True, vmem_limit_bytes=32 * 1024 * 1024
        ),
    )(
        index,
        tiles[0, 0],
        user_degree.reshape(n_col, user_group),
        item_degree.reshape(n_row, item_group),
        start_panel,
    )
    return tuple(out)


def solution(mesh):
    in_specs = (
        P("row", "col", None, None, None),
        P("row", "col", None),
        P("row", "col"),
        P("row"),
        P("col"),
        P(None, ("col", "row")),
    )
    out_specs = (P(None, ("row", "col")), P(None, ("col", "row")), P(), P())
    def whole(*args):
        tile_width = args[0].shape[3]
        cells = mesh.shape["row"] * mesh.shape["col"]
        owned = (args[3].shape[0] // cells, args[4].shape[0] // cells)
        form = per_device
        if owned[0] % tile_width or owned[1] % tile_width:
            form = per_device_arrays
        return jax.shard_map(
            form, mesh=mesh, in_specs=in_specs, out_specs=out_specs, check_vma=False
        )(*args)

    return whole
```

```python
import functools
import math

import jax
import jax.numpy as jnp
from jax import lax
from jax.experimental import pallas as pl
from jax.experimental.pallas import tpu as pltpu
from jax.sharding import PartitionSpec as P

STEPS = 3


HIGH = lax.Precision.HIGHEST


def gram_of(vectors):
    return jnp.einsum("bn,cn->bc", vectors, vectors, precision=HIGH)


def solve_lower(factor, vectors):
    return lax.linalg.triangular_solve(factor, vectors, left_side=True, lower=True)


def per_device_arrays(tiles, tile_slots, tile_counts, user_degree, item_degree, start_panel):
    tile_stack = tiles[0, 0].astype(jnp.float32)
    slot_list = tile_slots[0, 0]
    tile_total = tile_counts[0, 0]
    slot_count = tile_stack.shape[0]
    tile_width = tile_stack.shape[1]
    row_blocks = user_degree.shape[0] // tile_width
    col_blocks = item_degree.shape[0] // tile_width
    block_width = start_panel.shape[0]
    live_mask = jnp.arange(slot_count) < tile_total
    local_rows = slot_list // col_blocks
    local_cols = slot_list % col_blocks
    row_select = (
        (local_rows[:, None] == jnp.arange(row_blocks)[None, :]) & live_mask[:, None]
    ).astype(jnp.float32)
    col_select = (
        (local_cols[:, None] == jnp.arange(col_blocks)[None, :]) & live_mask[:, None]
    ).astype(jnp.float32)
    user_scale = lax.rsqrt(user_degree.astype(jnp.float32))
    item_scale = lax.rsqrt(item_degree.astype(jnp.float32))
    user_group = row_blocks * tile_width // lax.axis_size("col")
    item_group = col_blocks * tile_width // lax.axis_size("row")
    user_offset = lax.axis_index("col") * user_group
    item_offset = lax.axis_index("row") * item_group
    user_scale_own = lax.dynamic_slice_in_dim(user_scale, user_offset, user_group)
    item_scale_own = lax.dynamic_slice_in_dim(item_scale, item_offset, item_group)
    start_total = lax.psum(gram_of(start_panel), ("row", "col"))
    start_factor = jnp.linalg.cholesky(start_total)
    item_basis = solve_lower(start_factor, start_panel)
    user_basis = start_panel[:, :0]
    item_factor = start_factor
    user_list = []
    item_list = []
    for iteration in range(STEPS):
        scaled = item_basis * item_scale_own[None, :]
        item_full = lax.all_gather(scaled, "row", axis=1, tiled=True)
        forward_panel_blocks = item_full.reshape(block_width, col_blocks, tile_width)
        forward_chosen = jnp.take(forward_panel_blocks, local_cols, axis=1)
        forward_partial_value = jnp.einsum(
            "mrc,bmc->bmr", tile_stack, forward_chosen, precision=HIGH
        )
        forward_summed = jnp.einsum(
            "bmr,mk->bkr", forward_partial_value, row_select, precision=HIGH
        )
        forward = (
            lax.psum_scatter(
                forward_summed.reshape(block_width, row_blocks * tile_width),
                "col",
                scatter_dimension=1,
                tiled=True,
            )
            * user_scale_own[None, :]
        )
        if iteration > 0:
            forward = forward - jnp.dot(item_factor.T, user_basis, precision=HIGH)
        user_factor = jnp.linalg.cholesky(lax.psum(gram_of(forward), ("row", "col")))
        user_basis = solve_lower(user_factor, forward)
        scaled = user_basis * user_scale_own[None, :]
        user_full = lax.all_gather(scaled, "col", axis=1, tiled=True)
        panel_blocks = user_full.reshape(block_width, row_blocks, tile_width)
        chosen = jnp.take(panel_blocks, local_rows, axis=1)
        partial_value = jnp.einsum("mrc,bmr->bmc", tile_stack, chosen, precision=HIGH)
        summed = jnp.einsum("bmc,mk->bkc", partial_value, col_select, precision=HIGH)
        backward = (
            lax.psum_scatter(
                summed.reshape(block_width, col_blocks * tile_width),
                "row",
                scatter_dimension=1,
                tiled=True,
            )
            * item_scale_own[None, :]
        )
        backward = backward - jnp.dot(user_factor.T, item_basis, precision=HIGH)
        item_factor = jnp.linalg.cholesky(lax.psum(gram_of(backward), ("row", "col")))
        item_basis = solve_lower(item_factor, backward)
        user_list.append(user_factor)
        item_list.append(item_factor)
    user_total = row_blocks * tile_width * lax.axis_size("row")
    item_total = col_blocks * tile_width * lax.axis_size("col")
    return (
        math.sqrt(user_total) * user_basis,
        math.sqrt(item_total) * item_basis,
        jnp.stack(user_list),
        jnp.stack(item_list),
    )


MESH = pl.DeviceIdType.MESH
NT = (((1,), (1,)), ((), ()))
NN = (((1,), (0,)), ((), ()))


def dot_high(a, b, dims=NN):
    return lax.dot_general(
        a, b, dims, precision=HIGH, preferred_element_type=jnp.float32
    )


def factor_and_inverse(gram):
    n = gram.shape[0]
    blocks = n // 8
    eye = (
        lax.broadcasted_iota(jnp.int32, (n, n), 0)
        == lax.broadcasted_iota(jnp.int32, (n, n), 1)
    ).astype(jnp.float32)
    work = jnp.concatenate([gram, eye], axis=1)
    sub = lax.broadcasted_iota(jnp.int32, (8, 2 * n), 0)

    def block_step(b, parts):
        parts = list(parts)
        live = [None] + [
            (jnp.zeros((8, 2 * n), jnp.int32) + b < blocks - i).astype(jnp.float32)
            for i in range(1, blocks)
        ]
        head = parts[0]
        wide = (8, 2 * n)
        columns = [jnp.broadcast_to(head[:, s : s + 1], wide) for s in range(8)]
        others = [
            [jnp.broadcast_to(parts[i][:, s : s + 1], wide) * live[i] for s in range(8)]
            for i in range(1, blocks)
        ]
        for s in range(8):
            scale = lax.rsqrt(jnp.broadcast_to(columns[s][s : s + 1, :], wide))
            row = jnp.broadcast_to(head[s : s + 1, :], wide) * scale
            below = jnp.where(sub > s, columns[s] * scale, 0.0)
            head = jnp.where(sub == s, row, head - below * row)
            factors = [other[s] * scale for other in others]
            for t in range(s + 1, 8):
                across = jnp.broadcast_to(columns[t][s : s + 1, :], wide) * scale
                columns[t] = columns[t] - below * across
                for other, factor in zip(others, factors):
                    other[t] = other[t] - factor * across
            for i in range(1, blocks):
                parts[i] = parts[i] - factors[i - 1] * row
        parts[0] = head
        parts = [pltpu.roll(p, 2 * n - 8, 1) for p in parts]
        return tuple(parts[1:] + parts[:1])

    parts = tuple(work[8 * i : 8 * i + 8] for i in range(blocks))
    parts = lax.fori_loop(0, blocks, block_step, parts)
    work = jnp.concatenate(parts, axis=0)
    upper = lax.broadcasted_iota(jnp.int32, (n, n), 0) <= lax.broadcasted_iota(
        jnp.int32, (n, n), 1
    )
    return jnp.where(upper, work[:, n:], 0.0), work[:, :n]


def kernel(
    n_row,
    n_col,
    row_blocks,
    col_blocks,
    index_ref,
    tiles_ref,
    user_degree_ref,
    item_degree_ref,
    start_ref,
    left_ref,
    right_ref,
    left_factor_ref,
    right_factor_ref,
    item_all,
    user_all,
    split,
    running,
    user_send,
    sibling_in,
    user_send2,
    user_in,
    item_send,
    item_in,
    item_raw,
    item_basis,
    user_basis,
    gram_own,
    gram_row,
    gram_sum,
    gram_col,
    s_gr,
    r_gr,
    s_gc,
    r_gc,
    s_ir,
    r_ir,
    s_uz,
    r_uz,
    s_us,
    r_us,
    s_sib,
    r_sib,
    s_z,
    r_z,
    s_row,
    r_row,
):
    row = lax.axis_index("row")
    col = lax.axis_index("col")
    n_z = n_col // 2
    core = lax.rem(col, 2)
    z = col // 2
    sibling = col + 1 - 2 * core
    slots = tiles_ref.shape[0]
    width = tiles_ref.shape[1]
    block = start_ref.shape[0]
    half = block // 2
    user_group = user_all.shape[2]
    item_group = item_all.shape[2]
    user_per = user_group // width
    item_per = item_group // width

    barrier = pltpu.get_barrier_semaphore()
    for d in range(1, n_row):
        pl.semaphore_signal(
            barrier, inc=1, device_id=(lax.rem(row + d, n_row), col), device_id_type=MESH
        )
    for d in range(1, n_col):
        pl.semaphore_signal(
            barrier, inc=1, device_id=(row, lax.rem(col + d, n_col)), device_id_type=MESH
        )
    pl.semaphore_wait(barrier, n_row + n_col - 2)

    def send(src, dst, s_sem, r_sem, target):
        copy = pltpu.make_async_remote_copy(
            src_ref=src,
            dst_ref=dst,
            send_sem=s_sem,
            recv_sem=r_sem,
            device_id=target,
            device_id_type=MESH,
        )
        copy.start()
        return copy

    user_scale = lax.rsqrt(user_degree_ref[pl.ds(col, 1), :].astype(jnp.float32))
    item_scale = lax.rsqrt(item_degree_ref[pl.ds(row, 1), :].astype(jnp.float32))

    def gram_start(raw, way):
        gram = dot_high(raw, raw, NT)
        gram_own[way] = jnp.concatenate([gram[:half], gram[half:]], axis=1)
        copies = []
        for d in range(1, n_row):
            copies.append(
                send(
                    gram_own.at[way],
                    gram_row.at[way, d],
                    s_gr.at[way, d],
                    r_gr.at[way, d],
                    (lax.rem(row + d, n_row), col),
                )
            )
        return copies

    def gram_middle(copies, way):
        gram_row[way, 0] = gram_own[way]
        for copy in copies:
            copy.wait_recv()
        total = gram_row[way, row]
        for i in range(1, n_row):
            total = total + gram_row[way, lax.rem(row - i + n_row, n_row)]
        gram_sum[way] = total
        out = []
        for d in range(1, n_col):
            out.append(
                send(
                    gram_sum.at[way],
                    gram_col.at[way, d],
                    s_gc.at[way, d],
                    r_gc.at[way, d],
                    (row, lax.rem(col + d, n_col)),
                )
            )
        return out

    def gram_end(copies, way):
        for copy in copies:
            copy.wait_recv()
        total = jnp.zeros((half, 2 * block), jnp.float32)
        gram_col[way, 0] = gram_sum[way]
        for j in range(n_col):
            total = total + gram_col[way, lax.rem(col - j + n_col, n_col)]
        gram = jnp.concatenate([total[:, :block], total[:, block:]], axis=0)
        return factor_and_inverse(gram)

    def put_split(first_block, values):
        for b in range(values.shape[1] // width):
            part = values[:, b * width : (b + 1) * width]
            high = part.astype(jnp.bfloat16)
            low = (part - high.astype(jnp.float32)).astype(jnp.bfloat16)
            split[first_block + b] = jnp.concatenate([high, low], axis=0)

    def products(base, dims):
        def one(t, total):
            tile = tiles_ref[index_ref[base + t]]
            vectors = split[index_ref[base + slots + t]]
            keep = index_ref[base + 2 * slots + t].astype(jnp.float32)
            both = lax.dot_general(
                vectors, tile, dims, preferred_element_type=jnp.float32
            )
            total = total * keep + (both[:block] + both[block:])
            running[t] = total
            return total

        lax.fori_loop(
            0, slots, one, jnp.zeros((block, width), jnp.float32), unroll=8
        )

    running[slots] = jnp.zeros((block, width), jnp.float32)
    forward_base = 0
    forward_last = 3 * slots
    backward_base = forward_last + row_blocks
    backward_last = backward_base + 3 * slots

    item_raw[...] = start_ref[...]
    user_basis[...] = jnp.zeros_like(user_basis)

    def step(k, carry):
        raw = item_raw[...]
        scaled = raw * item_scale
        item_all[row] = scaled
        moved = []
        for d in range(1, n_row):
            moved.append(
                send(
                    item_all.at[row],
                    item_all.at[row],
                    s_ir.at[d],
                    r_ir.at[d],
                    (lax.rem(row + d, n_row), col),
                )
            )
        sent = gram_start(raw, 0)
        put_split(row * item_per, scaled)
        for d in range(1, n_row):
            moved[d - 1].wait_recv()
            source = lax.rem(row - d + n_row, n_row)
            put_split(source * item_per, item_all[source])
        sent2 = gram_middle(sent, 0)
        products(forward_base, NT)
        pair = []
        for core_at in range(2):
            for z_at in range(n_z):
                for b in range(user_per):
                    user_send[core_at * n_z + z_at, :, b * width : (b + 1) * width] = (
                        running[
                            index_ref[
                                forward_last + (z_at * 2 + core_at) * user_per + b
                            ]
                        ]
                    )
        for d in list(range(1, n_z)) + [0]:
            target_z = lax.rem(z + d, n_z)
            pair.append(
                send(
                    user_send.at[(1 - core) * n_z + target_z],
                    sibling_in.at[target_z],
                    s_sib.at[d],
                    r_sib.at[d],
                    (row, sibling),
                )
            )
        across = []
        for d in range(1, n_z):
            target_z = lax.rem(z + d, n_z)
            pair[d - 1].wait_recv()
            user_send2[target_z] = (
                user_send[core * n_z + target_z] + sibling_in[target_z]
            )
            across.append(
                send(
                    user_send2.at[target_z],
                    user_in.at[z],
                    s_z.at[d],
                    r_z.at[d],
                    (row, target_z * 2 + core),
                )
            )
        pair[n_z - 1].wait_recv()
        summed = user_send[core * n_z + z] + sibling_in[z]
        factor_t, inverse = gram_end(sent2, 0)
        right_factor_ref[lax.rem(k + STEPS - 1, STEPS)] = factor_t.T
        item_basis[...] = dot_high(inverse, raw)
        correction = dot_high(factor_t, user_basis[...])
        for d in range(1, n_z):
            across[d - 1].wait_recv()
            summed = summed + user_in[lax.rem(z - d + n_z, n_z)]
        forward = dot_high(inverse, summed * user_scale) - correction
        for copy in sent + sent2 + moved + pair + across:
            copy.wait_send()

        scaled = forward * user_scale
        user_all[col] = scaled
        moved = []
        for d in range(1, n_z):
            moved.append(
                send(
                    user_all.at[col],
                    user_all.at[col],
                    s_uz.at[d],
                    r_uz.at[d],
                    (row, lax.rem(z + d, n_z) * 2 + core),
                )
            )
        passed = [
            send(
                user_all.at[col],
                user_all.at[col],
                s_us.at[0],
                r_us.at[0],
                (row, sibling),
            )
        ]
        sent = gram_start(forward, 1)
        put_split(col * user_per, scaled)
        sent2 = gram_middle(sent, 1)
        passed[0].wait_recv()
        put_split(sibling * user_per, user_all[sibling])
        for d in range(1, n_z):
            moved[d - 1].wait_recv()
            source = lax.rem(z - d + n_z, n_z) * 2 + core
            passed.append(
                send(
                    user_all.at[source],
                    user_all.at[source],
                    s_us.at[d],
                    r_us.at[d],
                    (row, sibling),
                )
            )
            put_split(source * user_per, user_all[source])
        for d in range(1, n_z):
            passed[d].wait_recv()
            source = lax.rem(z - d + n_z, n_z) * 2 + 1 - core
            put_split(source * user_per, user_all[source])
        products(backward_base, NN)
        for j in range(n_row):
            for b in range(item_per):
                item_send[j, :, b * width : (b + 1) * width] = running[
                    index_ref[backward_last + j * item_per + b]
                ]
        across = []
        for d in range(1, n_row):
            target = lax.rem(row + d, n_row)
            across.append(
                send(
                    item_send.at[target],
                    item_in.at[row],
                    s_row.at[d],
                    r_row.at[d],
                    (target, col),
                )
            )
        factor_t, inverse = gram_end(sent2, 1)
        left_factor_ref[k] = factor_t.T
        user_basis[...] = dot_high(inverse, forward)
        correction = dot_high(factor_t, item_basis[...])
        summed = item_send[row]
        for d in range(1, n_row):
            across[d - 1].wait_recv()
            summed = summed + item_in[lax.rem(row - d + n_row, n_row)]
        item_raw[...] = dot_high(inverse, summed * item_scale) - correction
        for copy in sent + sent2 + moved + passed + across:
            copy.wait_send()
        return carry

    lax.fori_loop(0, STEPS, step, 0)

    raw = item_raw[...]
    sent = gram_start(raw, 0)
    left_ref[...] = user_basis[...] * math.sqrt(row_blocks * width * n_row)
    sent2 = gram_middle(sent, 0)
    factor_t, inverse = gram_end(sent2, 0)
    right_factor_ref[STEPS - 1] = factor_t.T
    right_ref[...] = dot_high(inverse, raw) * math.sqrt(col_blocks * width * n_col)
    for copy in sent + sent2:
        copy.wait_send()


def order_tables(keys, partners, live, blocks):
    slots = keys.shape[0]
    at = jnp.arange(slots)
    rank_key = jnp.where(live, keys, blocks) * slots + at
    rank = jnp.sum((rank_key[None, :] < rank_key[:, None]).astype(jnp.int32), axis=1)
    placed = rank[None, :] == at[:, None]
    order = jnp.sum(jnp.where(placed, at[None, :], 0), axis=1)
    partner = jnp.sum(jnp.where(placed, partners[None, :], 0), axis=1)
    same = (keys[None, :] == keys[:, None]) & (live[None, :] & live[:, None])
    earlier = jnp.any(same & (at[None, :] < at[:, None]), axis=1)
    keep = jnp.sum(jnp.where(placed, earlier[None, :].astype(jnp.int32), 0), axis=1)
    mine = (keys[None, :] == jnp.arange(blocks)[:, None]) & live[None, :]
    last = jnp.max(jnp.where(mine, rank[None, :], -1), axis=1)
    last = jnp.where(last < 0, slots, last)
    return [order, partner, keep, last]


def per_device(tiles, tile_slots, tile_counts, user_degree, item_degree, start_panel):
    n_row, n_col = lax.axis_size("row"), lax.axis_size("col")
    slots, width = tiles.shape[2], tiles.shape[3]
    block = start_panel.shape[0]
    row_blocks = user_degree.shape[0] // width
    col_blocks = item_degree.shape[0] // width
    user_group = user_degree.shape[0] // n_col
    item_group = item_degree.shape[0] // n_row
    slot_list = tile_slots[0, 0]
    live = jnp.arange(slots) < tile_counts[0, 0]
    slot_list = jnp.where(live, slot_list, 0)
    local_rows, local_cols = slot_list // col_blocks, slot_list % col_blocks
    index = jnp.concatenate(
        order_tables(local_rows, local_cols, live, row_blocks)
        + order_tables(local_cols, local_rows, live, col_blocks)
    ).astype(jnp.int32)
    vmem = pl.BlockSpec(memory_space=pltpu.VMEM)
    f32 = jnp.float32
    dma = pltpu.SemaphoreType.DMA
    n_z = n_col // 2
    out = pl.pallas_call(
        functools.partial(kernel, n_row, n_col, row_blocks, col_blocks),
        out_shape=(
            jax.ShapeDtypeStruct((block, user_group), f32),
            jax.ShapeDtypeStruct((block, item_group), f32),
            jax.ShapeDtypeStruct((STEPS, block, block), f32),
            jax.ShapeDtypeStruct((STEPS, block, block), f32),
        ),
        in_specs=[pl.BlockSpec(memory_space=pltpu.SMEM)] + [vmem] * 4,
        out_specs=(vmem,) * 4,
        scratch_shapes=[
            pltpu.VMEM((n_row, block, item_group), f32),
            pltpu.VMEM((n_col, block, user_group), f32),
            pltpu.VMEM((max(row_blocks, col_blocks), 2 * block, width), jnp.bfloat16),
            pltpu.VMEM((slots + 1, block, width), f32),
            pltpu.VMEM((n_col, block, user_group), f32),
            pltpu.VMEM((n_z, block, user_group), f32),
            pltpu.VMEM((n_z, block, user_group), f32),
            pltpu.VMEM((n_z, block, user_group), f32),
            pltpu.VMEM((n_row, block, item_group), f32),
            pltpu.VMEM((n_row, block, item_group), f32),
            pltpu.VMEM((block, item_group), f32),
            pltpu.VMEM((block, item_group), f32),
            pltpu.VMEM((block, user_group), f32),
            pltpu.VMEM((2, block // 2, 2 * block), f32),
            pltpu.VMEM((2, n_row, block // 2, 2 * block), f32),
            pltpu.VMEM((2, block // 2, 2 * block), f32),
            pltpu.VMEM((2, n_col, block // 2, 2 * block), f32),
            dma((2, n_row)),
            dma((2, n_row)),
            dma((2, n_col)),
            dma((2, n_col)),
            dma((n_row,)),
            dma((n_row,)),
            dma((n_z,)),
            dma((n_z,)),
            dma((n_z,)),
            dma((n_z,)),
            dma((n_z,)),
            dma((n_z,)),
            dma((n_z,)),
            dma((n_z,)),
            dma((n_row,)),
            dma((n_row,)),
        ],
        compiler_params=pltpu.CompilerParams(
            collective_id=0, has_side_effects=True, vmem_limit_bytes=32 * 1024 * 1024
        ),
    )(
        index,
        tiles[0, 0],
        user_degree.reshape(n_col, user_group),
        item_degree.reshape(n_row, item_group),
        start_panel,
    )
    return tuple(out)


def solution(mesh):
    in_specs = (
        P("row", "col", None, None, None),
        P("row", "col", None),
        P("row", "col"),
        P("row"),
        P("col"),
        P(None, ("col", "row")),
    )
    out_specs = (P(None, ("row", "col")), P(None, ("col", "row")), P(), P())
    def whole(*args):
        tile_width = args[0].shape[3]
        cells = mesh.shape["row"] * mesh.shape["col"]
        owned = (args[3].shape[0] // cells, args[4].shape[0] // cells)
        form = per_device
        if owned[0] % tile_width or owned[1] % tile_width:
            form = per_device_arrays
        return jax.shard_map(
            form, mesh=mesh, in_specs=in_specs, out_specs=out_specs, check_vma=False
        )(*args)

    return whole
```

```python
import functools
import math

import jax
import jax.numpy as jnp
from jax import lax
from jax.experimental import pallas as pl
from jax.experimental.pallas import tpu as pltpu
from jax.sharding import PartitionSpec as P

STEPS = 3


HIGH = lax.Precision.HIGHEST


def gram_of(vectors):
    return jnp.einsum("bn,cn->bc", vectors, vectors, precision=HIGH)


def solve_lower(factor, vectors):
    return lax.linalg.triangular_solve(factor, vectors, left_side=True, lower=True)


def per_device_arrays(tiles, tile_slots, tile_counts, user_degree, item_degree, start_panel):
    tile_stack = tiles[0, 0].astype(jnp.float32)
    slot_list = tile_slots[0, 0]
    tile_total = tile_counts[0, 0]
    slot_count = tile_stack.shape[0]
    tile_width = tile_stack.shape[1]
    row_blocks = user_degree.shape[0] // tile_width
    col_blocks = item_degree.shape[0] // tile_width
    block_width = start_panel.shape[0]
    live_mask = jnp.arange(slot_count) < tile_total
    local_rows = slot_list // col_blocks
    local_cols = slot_list % col_blocks
    row_select = (
        (local_rows[:, None] == jnp.arange(row_blocks)[None, :]) & live_mask[:, None]
    ).astype(jnp.float32)
    col_select = (
        (local_cols[:, None] == jnp.arange(col_blocks)[None, :]) & live_mask[:, None]
    ).astype(jnp.float32)
    user_scale = lax.rsqrt(user_degree.astype(jnp.float32))
    item_scale = lax.rsqrt(item_degree.astype(jnp.float32))
    user_group = row_blocks * tile_width // lax.axis_size("col")
    item_group = col_blocks * tile_width // lax.axis_size("row")
    user_offset = lax.axis_index("col") * user_group
    item_offset = lax.axis_index("row") * item_group
    user_scale_own = lax.dynamic_slice_in_dim(user_scale, user_offset, user_group)
    item_scale_own = lax.dynamic_slice_in_dim(item_scale, item_offset, item_group)
    start_total = lax.psum(gram_of(start_panel), ("row", "col"))
    start_factor = jnp.linalg.cholesky(start_total)
    item_basis = solve_lower(start_factor, start_panel)
    user_basis = start_panel[:, :0]
    item_factor = start_factor
    user_list = []
    item_list = []
    for iteration in range(STEPS):
        scaled = item_basis * item_scale_own[None, :]
        item_full = lax.all_gather(scaled, "row", axis=1, tiled=True)
        forward_panel_blocks = item_full.reshape(block_width, col_blocks, tile_width)
        forward_chosen = jnp.take(forward_panel_blocks, local_cols, axis=1)
        forward_partial_value = jnp.einsum(
            "mrc,bmc->bmr", tile_stack, forward_chosen, precision=HIGH
        )
        forward_summed = jnp.einsum(
            "bmr,mk->bkr", forward_partial_value, row_select, precision=HIGH
        )
        forward = (
            lax.psum_scatter(
                forward_summed.reshape(block_width, row_blocks * tile_width),
                "col",
                scatter_dimension=1,
                tiled=True,
            )
            * user_scale_own[None, :]
        )
        if iteration > 0:
            forward = forward - jnp.dot(item_factor.T, user_basis, precision=HIGH)
        user_factor = jnp.linalg.cholesky(lax.psum(gram_of(forward), ("row", "col")))
        user_basis = solve_lower(user_factor, forward)
        scaled = user_basis * user_scale_own[None, :]
        user_full = lax.all_gather(scaled, "col", axis=1, tiled=True)
        panel_blocks = user_full.reshape(block_width, row_blocks, tile_width)
        chosen = jnp.take(panel_blocks, local_rows, axis=1)
        partial_value = jnp.einsum("mrc,bmr->bmc", tile_stack, chosen, precision=HIGH)
        summed = jnp.einsum("bmc,mk->bkc", partial_value, col_select, precision=HIGH)
        backward = (
            lax.psum_scatter(
                summed.reshape(block_width, col_blocks * tile_width),
                "row",
                scatter_dimension=1,
                tiled=True,
            )
            * item_scale_own[None, :]
        )
        backward = backward - jnp.dot(user_factor.T, item_basis, precision=HIGH)
        item_factor = jnp.linalg.cholesky(lax.psum(gram_of(backward), ("row", "col")))
        item_basis = solve_lower(item_factor, backward)
        user_list.append(user_factor)
        item_list.append(item_factor)
    user_total = row_blocks * tile_width * lax.axis_size("row")
    item_total = col_blocks * tile_width * lax.axis_size("col")
    return (
        math.sqrt(user_total) * user_basis,
        math.sqrt(item_total) * item_basis,
        jnp.stack(user_list),
        jnp.stack(item_list),
    )


MESH = pl.DeviceIdType.MESH
NT = (((1,), (1,)), ((), ()))
NN = (((1,), (0,)), ((), ()))


def dot_high(a, b, dims=NN):
    return lax.dot_general(
        a, b, dims, precision=HIGH, preferred_element_type=jnp.float32
    )


def factor_and_inverse(gram):
    n = gram.shape[0]
    blocks = n // 8
    eye = (
        lax.broadcasted_iota(jnp.int32, (n, n), 0)
        == lax.broadcasted_iota(jnp.int32, (n, n), 1)
    ).astype(jnp.float32)
    work = jnp.concatenate([gram, eye], axis=1)
    sub = lax.broadcasted_iota(jnp.int32, (8, 2 * n), 0)

    def block_step(b, parts):
        parts = list(parts)
        live = [None] + [
            (jnp.zeros((8, 2 * n), jnp.int32) + b < blocks - i).astype(jnp.float32)
            for i in range(1, blocks)
        ]
        head = parts[0]
        wide = (8, 2 * n)
        columns = [jnp.broadcast_to(head[:, s : s + 1], wide) for s in range(8)]
        others = [
            [jnp.broadcast_to(parts[i][:, s : s + 1], wide) * live[i] for s in range(8)]
            for i in range(1, blocks)
        ]
        for s in range(8):
            scale = lax.rsqrt(jnp.broadcast_to(columns[s][s : s + 1, :], wide))
            row = jnp.broadcast_to(head[s : s + 1, :], wide) * scale
            below = jnp.where(sub > s, columns[s] * scale, 0.0)
            head = jnp.where(sub == s, row, head - below * row)
            factors = [other[s] * scale for other in others]
            for t in range(s + 1, 8):
                across = jnp.broadcast_to(columns[t][s : s + 1, :], wide) * scale
                columns[t] = columns[t] - below * across
                for other, factor in zip(others, factors):
                    other[t] = other[t] - factor * across
            for i in range(1, blocks):
                parts[i] = parts[i] - factors[i - 1] * row
        parts[0] = head
        parts = [pltpu.roll(p, 2 * n - 8, 1) for p in parts]
        return tuple(parts[1:] + parts[:1])

    parts = tuple(work[8 * i : 8 * i + 8] for i in range(blocks))
    parts = lax.fori_loop(0, blocks, block_step, parts)
    work = jnp.concatenate(parts, axis=0)
    upper = lax.broadcasted_iota(jnp.int32, (n, n), 0) <= lax.broadcasted_iota(
        jnp.int32, (n, n), 1
    )
    return jnp.where(upper, work[:, n:], 0.0), work[:, :n]


def kernel(
    n_row,
    n_col,
    row_blocks,
    col_blocks,
    index_ref,
    tiles_hbm,
    user_degree_ref,
    item_degree_ref,
    start_hbm,
    left_ref,
    right_ref,
    left_factor_ref,
    right_factor_ref,
    tiles_ref,
    item_all,
    user_all,
    split,
    running,
    user_send,
    sibling_in,
    user_send2,
    user_in,
    item_send,
    item_in,
    item_raw,
    item_basis,
    user_basis,
    gram_own,
    gram_row,
    gram_sum,
    gram_col,
    gram_all,
    s_in,
    s_gr,
    r_gr,
    s_gc,
    r_gc,
    s_ga,
    r_ga,
    s_ir,
    r_ir,
    s_uz,
    r_uz,
    s_us,
    r_us,
    s_sib,
    r_sib,
    s_z,
    r_z,
    s_row,
    r_row,
):
    row = lax.axis_index("row")
    col = lax.axis_index("col")
    n_z = n_col // 2
    core = lax.rem(col, 2)
    z = col // 2
    sibling = col + 1 - 2 * core
    slots = tiles_ref.shape[0]
    width = tiles_ref.shape[1]
    block = item_raw.shape[0]
    half = block // 2
    part = half // n_row
    user_group = user_all.shape[3]
    item_group = item_all.shape[3]
    user_per = user_group // width
    item_per = item_group // width

    start_in = pltpu.make_async_copy(start_hbm, item_raw, s_in.at[0])
    start_in.start()
    tiles_in = pltpu.make_async_copy(tiles_hbm, tiles_ref, s_in.at[1])
    tiles_in.start()

    barrier = pltpu.get_barrier_semaphore()
    for d in range(1, n_row):
        pl.semaphore_signal(
            barrier, inc=1, device_id=(lax.rem(row + d, n_row), col), device_id_type=MESH
        )
    for d in range(1, n_col):
        pl.semaphore_signal(
            barrier, inc=1, device_id=(row, lax.rem(col + d, n_col)), device_id_type=MESH
        )

    def send(src, dst, s_sem, r_sem, target):
        copy = pltpu.make_async_remote_copy(
            src_ref=src,
            dst_ref=dst,
            send_sem=s_sem,
            recv_sem=r_sem,
            device_id=target,
            device_id_type=MESH,
        )
        copy.start()
        return copy

    user_scale = lax.rsqrt(user_degree_ref[pl.ds(col, 1), :].astype(jnp.float32))
    item_scale = lax.rsqrt(item_degree_ref[pl.ds(row, 1), :].astype(jnp.float32))

    def gram_start(raw, way):
        gram = dot_high(raw, raw, NT)
        packed = jnp.concatenate([gram[:half], gram[half:]], axis=1)
        for i in range(n_row):
            gram_own[way, i] = packed[i * part : (i + 1) * part]
        copies = []
        for d in range(1, n_row):
            target = lax.rem(row + d, n_row)
            copies.append(
                send(
                    gram_own.at[way, target],
                    gram_row.at[way, d],
                    s_gr.at[way, d],
                    r_gr.at[way, d],
                    (target, col),
                )
            )
        return copies

    def gram_middle(copies, way):
        total = gram_own[way, row]
        for d in range(1, n_row):
            copies[d - 1].wait_recv()
            total = total + gram_row[way, d]
        gram_sum[way] = total
        out = []
        for d in range(1, n_col):
            out.append(
                send(
                    gram_sum.at[way],
                    gram_col.at[way, d],
                    s_gc.at[way, d],
                    r_gc.at[way, d],
                    (row, lax.rem(col + d, n_col)),
                )
            )
        return out

    def gram_late(copies, way):
        for copy in copies:
            copy.wait_recv()
        gram_col[way, 0] = gram_sum[way]
        total = gram_col[way, col]
        for j in range(1, n_col):
            total = total + gram_col[way, lax.rem(col - j + n_col, n_col)]
        gram_all[way, row] = total
        out = []
        for d in range(1, n_row):
            out.append(
                send(
                    gram_all.at[way, row],
                    gram_all.at[way, row],
                    s_ga.at[way, d],
                    r_ga.at[way, d],
                    (lax.rem(row + d, n_row), col),
                )
            )
        return out

    def gram_end(copies, way):
        for copy in copies:
            copy.wait_recv()
        total = jnp.concatenate([gram_all[way, i] for i in range(n_row)], axis=0)
        gram = jnp.concatenate([total[:, :block], total[:, block:]], axis=0)
        return factor_and_inverse(gram)

    def put_split(h, first_block, values):
        for b in range(values.shape[1] // width):
            piece = values[:, b * width : (b + 1) * width]
            high = piece.astype(jnp.bfloat16)
            low = (piece - high.astype(jnp.float32)).astype(jnp.bfloat16)
            split[h, first_block + b] = jnp.concatenate([high, low], axis=0)

    def products(h, base, dims):
        def one(t, total):
            tile = tiles_ref[index_ref[base + t]]
            vectors = split[h, index_ref[base + slots + t]]
            keep = index_ref[base + 2 * slots + t].astype(jnp.float32)
            both = lax.dot_general(
                vectors, tile, dims, preferred_element_type=jnp.float32
            )
            total = total * keep + (both[:half] + both[half:])
            running[h, t] = total
            return total

        lax.fori_loop(0, slots, one, jnp.zeros((half, width), jnp.float32), unroll=8)

    forward_base = 0
    forward_last = 3 * slots
    backward_base = forward_last + row_blocks
    backward_last = backward_base + 3 * slots

    for h in range(2):
        running[h, slots] = jnp.zeros((half, width), jnp.float32)
    user_basis[...] = jnp.zeros_like(user_basis)
    start_in.wait()
    pl.semaphore_wait(barrier, n_row + n_col - 2)
    tiles_in.wait()

    def step(k, carry):
        raw = item_raw[...]
        scaled = raw * item_scale
        moved = [[], []]

        def send_items(h):
            item_all[h, row] = scaled[h * half : (h + 1) * half]
            for d in range(1, n_row):
                moved[h].append(
                    send(
                        item_all.at[h, row],
                        item_all.at[h, row],
                        s_ir.at[h, d],
                        r_ir.at[h, d],
                        (lax.rem(row + d, n_row), col),
                    )
                )

        def take_items(h):
            for d in range(1, n_row):
                moved[h][d - 1].wait_recv()
                source = lax.rem(row - d + n_row, n_row)
                put_split(h, source * item_per, item_all[h, source])

        pair = [[], []]
        across = [[], []]

        def send_pair(h):
            for core_at in range(2):
                for z_at in range(n_z):
                    for b in range(user_per):
                        owned = (z_at * 2 + core_at) * user_per + b
                        user_send[
                            h, core_at * n_z + z_at, :, b * width : (b + 1) * width
                        ] = running[h, index_ref[forward_last + owned]]
            for d in list(range(1, n_z)) + [0]:
                target_z = lax.rem(z + d, n_z)
                pair[h].append(
                    send(
                        user_send.at[h, (1 - core) * n_z + target_z],
                        sibling_in.at[h, target_z],
                        s_sib.at[h, d],
                        r_sib.at[h, d],
                        (row, sibling),
                    )
                )

        def send_across(h):
            for d in range(1, n_z):
                target_z = lax.rem(z + d, n_z)
                pair[h][d - 1].wait_recv()
                user_send2[h, target_z] = (
                    user_send[h, core * n_z + target_z] + sibling_in[h, target_z]
                )
                across[h].append(
                    send(
                        user_send2.at[h, target_z],
                        user_in.at[h, z],
                        s_z.at[h, d],
                        r_z.at[h, d],
                        (row, target_z * 2 + core),
                    )
                )
            pair[h][n_z - 1].wait_recv()
            return user_send[h, core * n_z + z] + sibling_in[h, z]

        send_items(0)
        sent = gram_start(raw, 0)
        send_items(1)
        for h in range(2):
            put_split(h, row * item_per, scaled[h * half : (h + 1) * half])
        take_items(0)
        sent2 = gram_middle(sent, 0)
        products(0, forward_base, NT)
        send_pair(0)
        take_items(1)
        summed0 = send_across(0)
        products(1, forward_base, NT)
        send_pair(1)
        sent3 = gram_late(sent2, 0)
        summed1 = send_across(1)
        factor_t, inverse = gram_end(sent3, 0)
        right_factor_ref[lax.rem(k + STEPS - 1, STEPS)] = factor_t.T
        item_basis[...] = dot_high(inverse, raw)
        correction = dot_high(factor_t, user_basis[...])
        sums = [summed0, summed1]
        for h in range(2):
            for d in range(1, n_z):
                across[h][d - 1].wait_recv()
                sums[h] = sums[h] + user_in[h, lax.rem(z - d + n_z, n_z)]
        summed = jnp.concatenate(sums, axis=0)
        forward = dot_high(inverse, summed * user_scale) - correction
        for group in [sent, sent2, sent3] + moved + pair + across:
            for copy in group:
                copy.wait_send()

        scaled = forward * user_scale
        moved_u = [[], []]
        passed = [[], []]

        def send_users(h):
            user_all[h, col] = scaled[h * half : (h + 1) * half]
            for d in range(1, n_z):
                moved_u[h].append(
                    send(
                        user_all.at[h, col],
                        user_all.at[h, col],
                        s_uz.at[h, d],
                        r_uz.at[h, d],
                        (row, lax.rem(z + d, n_z) * 2 + core),
                    )
                )
            pass_on(h, col, 0)

        def pass_on(h, source, d):
            passed[h].append(
                send(
                    user_all.at[h, source],
                    user_all.at[h, source],
                    s_us.at[h, d],
                    r_us.at[h, d],
                    (row, sibling),
                )
            )

        def take_users(h):
            passed[h][0].wait_recv()
            put_split(h, sibling * user_per, user_all[h, sibling])
            for d in range(1, n_z):
                moved_u[h][d - 1].wait_recv()
                source = lax.rem(z - d + n_z, n_z) * 2 + core
                pass_on(h, source, d)
                put_split(h, source * user_per, user_all[h, source])
            for d in range(1, n_z):
                passed[h][d].wait_recv()
                source = lax.rem(z - d + n_z, n_z) * 2 + 1 - core
                put_split(h, source * user_per, user_all[h, source])

        back = [[], []]

        def send_rows(h):
            for j in range(n_row):
                for b in range(item_per):
                    item_send[h, j, :, b * width : (b + 1) * width] = running[
                        h, index_ref[backward_last + j * item_per + b]
                    ]
            for d in range(1, n_row):
                target = lax.rem(row + d, n_row)
                back[h].append(
                    send(
                        item_send.at[h, target],
                        item_in.at[h, row],
                        s_row.at[h, d],
                        r_row.at[h, d],
                        (target, col),
                    )
                )

        send_users(0)
        sent = gram_start(forward, 1)
        send_users(1)
        for h in range(2):
            put_split(h, col * user_per, scaled[h * half : (h + 1) * half])
        sent2 = gram_middle(sent, 1)
        take_users(0)
        products(0, backward_base, NN)
        send_rows(0)
        sent3 = gram_late(sent2, 1)
        take_users(1)
        products(1, backward_base, NN)
        send_rows(1)
        factor_t, inverse = gram_end(sent3, 1)
        left_factor_ref[k] = factor_t.T
        user_basis[...] = dot_high(inverse, forward)
        correction = dot_high(factor_t, item_basis[...])
        sums = []
        for h in range(2):
            total = item_send[h, row]
            for d in range(1, n_row):
                back[h][d - 1].wait_recv()
                total = total + item_in[h, lax.rem(row - d + n_row, n_row)]
            sums.append(total)
        summed = jnp.concatenate(sums, axis=0)
        item_raw[...] = dot_high(inverse, summed * item_scale) - correction
        for group in [sent, sent2, sent3] + moved_u + passed + back:
            for copy in group:
                copy.wait_send()
        return carry

    lax.fori_loop(0, STEPS, step, 0)

    raw = item_raw[...]
    sent = gram_start(raw, 0)
    left_ref[...] = user_basis[...] * math.sqrt(row_blocks * width * n_row)
    sent2 = gram_middle(sent, 0)
    sent3 = gram_late(sent2, 0)
    factor_t, inverse = gram_end(sent3, 0)
    right_factor_ref[STEPS - 1] = factor_t.T
    right_ref[...] = dot_high(inverse, raw) * math.sqrt(col_blocks * width * n_col)
    for copy in sent + sent2 + sent3:
        copy.wait_send()


def order_tables(keys, partners, live, blocks):
    slots = keys.shape[0]
    at = jnp.arange(slots)
    rank_key = jnp.where(live, keys, blocks) * slots + at
    rank = jnp.sum((rank_key[None, :] < rank_key[:, None]).astype(jnp.int32), axis=1)
    placed = rank[None, :] == at[:, None]
    order = jnp.sum(jnp.where(placed, at[None, :], 0), axis=1)
    partner = jnp.sum(jnp.where(placed, partners[None, :], 0), axis=1)
    same = (keys[None, :] == keys[:, None]) & (live[None, :] & live[:, None])
    earlier = jnp.any(same & (at[None, :] < at[:, None]), axis=1)
    keep = jnp.sum(jnp.where(placed, earlier[None, :].astype(jnp.int32), 0), axis=1)
    mine = (keys[None, :] == jnp.arange(blocks)[:, None]) & live[None, :]
    last = jnp.max(jnp.where(mine, rank[None, :], -1), axis=1)
    last = jnp.where(last < 0, slots, last)
    return [order, partner, keep, last]


def per_device(tiles, tile_slots, tile_counts, user_degree, item_degree, start_panel):
    n_row, n_col = lax.axis_size("row"), lax.axis_size("col")
    slots, width = tiles.shape[2], tiles.shape[3]
    block = start_panel.shape[0]
    row_blocks = user_degree.shape[0] // width
    col_blocks = item_degree.shape[0] // width
    user_group = user_degree.shape[0] // n_col
    item_group = item_degree.shape[0] // n_row
    slot_list = tile_slots[0, 0]
    live = jnp.arange(slots) < tile_counts[0, 0]
    slot_list = jnp.where(live, slot_list, 0)
    local_rows, local_cols = slot_list // col_blocks, slot_list % col_blocks
    index = jnp.concatenate(
        order_tables(local_rows, local_cols, live, row_blocks)
        + order_tables(local_cols, local_rows, live, col_blocks)
    ).astype(jnp.int32)
    vmem = pl.BlockSpec(memory_space=pltpu.VMEM)
    f32 = jnp.float32
    dma = pltpu.SemaphoreType.DMA
    n_z = n_col // 2
    half = block // 2
    part = half // n_row
    anywhere = pl.BlockSpec(memory_space=pl.ANY)
    out = pl.pallas_call(
        functools.partial(kernel, n_row, n_col, row_blocks, col_blocks),
        out_shape=(
            jax.ShapeDtypeStruct((block, user_group), f32),
            jax.ShapeDtypeStruct((block, item_group), f32),
            jax.ShapeDtypeStruct((STEPS, block, block), f32),
            jax.ShapeDtypeStruct((STEPS, block, block), f32),
        ),
        in_specs=[pl.BlockSpec(memory_space=pltpu.SMEM), anywhere, vmem, vmem, anywhere],
        out_specs=(vmem,) * 4,
        scratch_shapes=[
            pltpu.VMEM((slots, width, width), tiles.dtype),
            pltpu.VMEM((2, n_row, half, item_group), f32),
            pltpu.VMEM((2, n_col, half, user_group), f32),
            pltpu.VMEM((2, max(row_blocks, col_blocks), block, width), jnp.bfloat16),
            pltpu.VMEM((2, slots + 1, half, width), f32),
            pltpu.VMEM((2, n_col, half, user_group), f32),
            pltpu.VMEM((2, n_z, half, user_group), f32),
            pltpu.VMEM((2, n_z, half, user_group), f32),
            pltpu.VMEM((2, n_z, half, user_group), f32),
            pltpu.VMEM((2, n_row, half, item_group), f32),
            pltpu.VMEM((2, n_row, half, item_group), f32),
            pltpu.VMEM((block, item_group), f32),
            pltpu.VMEM((block, item_group), f32),
            pltpu.VMEM((block, user_group), f32),
            pltpu.VMEM((2, n_row, part, 2 * block), f32),
            pltpu.VMEM((2, n_row, part, 2 * block), f32),
            pltpu.VMEM((2, part, 2 * block), f32),
            pltpu.VMEM((2, n_col, part, 2 * block), f32),
            pltpu.VMEM((2, n_row, part, 2 * block), f32),
            dma((2,)),
            dma((2, n_row)),
            dma((2, n_row)),
            dma((2, n_col)),
            dma((2, n_col)),
            dma((2, n_row)),
            dma((2, n_row)),
            dma((2, n_row)),
            dma((2, n_row)),
            dma((2, n_z)),
            dma((2, n_z)),
            dma((2, n_z)),
            dma((2, n_z)),
            dma((2, n_z)),
            dma((2, n_z)),
            dma((2, n_z)),
            dma((2, n_z)),
            dma((2, n_row)),
            dma((2, n_row)),
        ],
        compiler_params=pltpu.CompilerParams(
            collective_id=0, has_side_effects=True, vmem_limit_bytes=32 * 1024 * 1024
        ),
    )(
        index,
        tiles[0, 0],
        user_degree.reshape(n_col, user_group),
        item_degree.reshape(n_row, item_group),
        start_panel,
    )
    return tuple(out)


def solution(mesh):
    in_specs = (
        P("row", "col", None, None, None),
        P("row", "col", None),
        P("row", "col"),
        P("row"),
        P("col"),
        P(None, ("col", "row")),
    )
    out_specs = (P(None, ("row", "col")), P(None, ("col", "row")), P(), P())
    def whole(*args):
        tile_width = args[0].shape[3]
        cells = mesh.shape["row"] * mesh.shape["col"]
        owned = (args[3].shape[0] // cells, args[4].shape[0] // cells)
        form = per_device
        sliver = (args[5].shape[0] // 2) % (8 * mesh.shape["row"])
        if owned[0] % tile_width or owned[1] % tile_width or sliver:
            form = per_device_arrays
        return jax.shard_map(
            form, mesh=mesh, in_specs=in_specs, out_specs=out_specs, check_vma=False
        )(*args)

    return whole
```

```python
import functools
import math

import jax
import jax.numpy as jnp
from jax import lax
from jax.experimental import pallas as pl
from jax.experimental.pallas import tpu as pltpu
from jax.sharding import PartitionSpec as P

STEPS = 3


HIGH = lax.Precision.HIGHEST


def gram_of(vectors):
    return jnp.einsum("bn,cn->bc", vectors, vectors, precision=HIGH)


def solve_lower(factor, vectors):
    return lax.linalg.triangular_solve(factor, vectors, left_side=True, lower=True)


def per_device_arrays(tiles, tile_slots, tile_counts, user_degree, item_degree, start_panel):
    tile_stack = tiles[0, 0].astype(jnp.float32)
    slot_list = tile_slots[0, 0]
    tile_total = tile_counts[0, 0]
    slot_count = tile_stack.shape[0]
    tile_width = tile_stack.shape[1]
    row_blocks = user_degree.shape[0] // tile_width
    col_blocks = item_degree.shape[0] // tile_width
    block_width = start_panel.shape[0]
    live_mask = jnp.arange(slot_count) < tile_total
    local_rows = slot_list // col_blocks
    local_cols = slot_list % col_blocks
    row_select = (
        (local_rows[:, None] == jnp.arange(row_blocks)[None, :]) & live_mask[:, None]
    ).astype(jnp.float32)
    col_select = (
        (local_cols[:, None] == jnp.arange(col_blocks)[None, :]) & live_mask[:, None]
    ).astype(jnp.float32)
    user_scale = lax.rsqrt(user_degree.astype(jnp.float32))
    item_scale = lax.rsqrt(item_degree.astype(jnp.float32))
    user_group = row_blocks * tile_width // lax.axis_size("col")
    item_group = col_blocks * tile_width // lax.axis_size("row")
    user_offset = lax.axis_index("col") * user_group
    item_offset = lax.axis_index("row") * item_group
    user_scale_own = lax.dynamic_slice_in_dim(user_scale, user_offset, user_group)
    item_scale_own = lax.dynamic_slice_in_dim(item_scale, item_offset, item_group)
    start_total = lax.psum(gram_of(start_panel), ("row", "col"))
    start_factor = jnp.linalg.cholesky(start_total)
    item_basis = solve_lower(start_factor, start_panel)
    user_basis = start_panel[:, :0]
    item_factor = start_factor
    user_list = []
    item_list = []
    for iteration in range(STEPS):
        scaled = item_basis * item_scale_own[None, :]
        item_full = lax.all_gather(scaled, "row", axis=1, tiled=True)
        forward_panel_blocks = item_full.reshape(block_width, col_blocks, tile_width)
        forward_chosen = jnp.take(forward_panel_blocks, local_cols, axis=1)
        forward_partial_value = jnp.einsum(
            "mrc,bmc->bmr", tile_stack, forward_chosen, precision=HIGH
        )
        forward_summed = jnp.einsum(
            "bmr,mk->bkr", forward_partial_value, row_select, precision=HIGH
        )
        forward = (
            lax.psum_scatter(
                forward_summed.reshape(block_width, row_blocks * tile_width),
                "col",
                scatter_dimension=1,
                tiled=True,
            )
            * user_scale_own[None, :]
        )
        if iteration > 0:
            forward = forward - jnp.dot(item_factor.T, user_basis, precision=HIGH)
        user_factor = jnp.linalg.cholesky(lax.psum(gram_of(forward), ("row", "col")))
        user_basis = solve_lower(user_factor, forward)
        scaled = user_basis * user_scale_own[None, :]
        user_full = lax.all_gather(scaled, "col", axis=1, tiled=True)
        panel_blocks = user_full.reshape(block_width, row_blocks, tile_width)
        chosen = jnp.take(panel_blocks, local_rows, axis=1)
        partial_value = jnp.einsum("mrc,bmr->bmc", tile_stack, chosen, precision=HIGH)
        summed = jnp.einsum("bmc,mk->bkc", partial_value, col_select, precision=HIGH)
        backward = (
            lax.psum_scatter(
                summed.reshape(block_width, col_blocks * tile_width),
                "row",
                scatter_dimension=1,
                tiled=True,
            )
            * item_scale_own[None, :]
        )
        backward = backward - jnp.dot(user_factor.T, item_basis, precision=HIGH)
        item_factor = jnp.linalg.cholesky(lax.psum(gram_of(backward), ("row", "col")))
        item_basis = solve_lower(item_factor, backward)
        user_list.append(user_factor)
        item_list.append(item_factor)
    user_total = row_blocks * tile_width * lax.axis_size("row")
    item_total = col_blocks * tile_width * lax.axis_size("col")
    return (
        math.sqrt(user_total) * user_basis,
        math.sqrt(item_total) * item_basis,
        jnp.stack(user_list),
        jnp.stack(item_list),
    )


MESH = pl.DeviceIdType.MESH
NT = (((1,), (1,)), ((), ()))
NN = (((1,), (0,)), ((), ()))


def dot_high(a, b, dims=NN):
    return lax.dot_general(
        a, b, dims, precision=HIGH, preferred_element_type=jnp.float32
    )


def factor_and_inverse(gram):
    n = gram.shape[0]
    blocks = n // 8
    eye = (
        lax.broadcasted_iota(jnp.int32, (n, n), 0)
        == lax.broadcasted_iota(jnp.int32, (n, n), 1)
    ).astype(jnp.float32)
    work = jnp.concatenate([gram, eye], axis=1)
    sub = lax.broadcasted_iota(jnp.int32, (8, 2 * n), 0)

    def block_step(b, parts):
        parts = list(parts)
        live = [None] + [
            (jnp.zeros((8, 2 * n), jnp.int32) + b < blocks - i).astype(jnp.float32)
            for i in range(1, blocks)
        ]
        head = parts[0]
        wide = (8, 2 * n)
        columns = [jnp.broadcast_to(head[:, s : s + 1], wide) for s in range(8)]
        others = [
            [jnp.broadcast_to(parts[i][:, s : s + 1], wide) * live[i] for s in range(8)]
            for i in range(1, blocks)
        ]
        for s in range(8):
            scale = lax.rsqrt(jnp.broadcast_to(columns[s][s : s + 1, :], wide))
            row = jnp.broadcast_to(head[s : s + 1, :], wide) * scale
            below = jnp.where(sub > s, columns[s] * scale, 0.0)
            head = jnp.where(sub == s, row, head - below * row)
            factors = [other[s] * scale for other in others]
            for t in range(s + 1, 8):
                across = jnp.broadcast_to(columns[t][s : s + 1, :], wide) * scale
                columns[t] = columns[t] - below * across
                for other, factor in zip(others, factors):
                    other[t] = other[t] - factor * across
            for i in range(1, blocks):
                parts[i] = parts[i] - factors[i - 1] * row
        parts[0] = head
        parts = [pltpu.roll(p, 2 * n - 8, 1) for p in parts]
        return tuple(parts[1:] + parts[:1])

    parts = tuple(work[8 * i : 8 * i + 8] for i in range(blocks))
    parts = lax.fori_loop(0, blocks, block_step, parts)
    work = jnp.concatenate(parts, axis=0)
    upper = lax.broadcasted_iota(jnp.int32, (n, n), 0) <= lax.broadcasted_iota(
        jnp.int32, (n, n), 1
    )
    return jnp.where(upper, work[:, n:], 0.0), work[:, :n]


def kernel(
    n_row,
    n_col,
    row_blocks,
    col_blocks,
    index_ref,
    tiles_hbm,
    user_degree_ref,
    item_degree_ref,
    start_hbm,
    left_ref,
    right_ref,
    left_factor_ref,
    right_factor_ref,
    tiles_ref,
    item_all,
    user_all,
    split,
    running,
    user_send,
    sibling_in,
    user_send2,
    user_in,
    item_send,
    item_in,
    item_raw,
    item_basis,
    user_basis,
    gram_own,
    gram_row,
    gram_sum,
    gram_col,
    gram_all,
    s_in,
    s_gr,
    r_gr,
    s_gc,
    r_gc,
    s_ga,
    r_ga,
    s_ir,
    r_ir,
    s_uz,
    r_uz,
    s_us,
    r_us,
    s_sib,
    r_sib,
    s_z,
    r_z,
    s_row,
    r_row,
):
    row = lax.axis_index("row")
    col = lax.axis_index("col")
    n_z = n_col // 2
    core = lax.rem(col, 2)
    z = col // 2
    sibling = col + 1 - 2 * core
    slots = tiles_ref.shape[0]
    width = tiles_ref.shape[1]
    block = item_raw.shape[0]
    half = block // 2
    part = half // n_row
    user_group = user_all.shape[3]
    item_group = item_all.shape[3]
    user_per = user_group // width
    item_per = item_group // width

    start_in = pltpu.make_async_copy(start_hbm, item_raw, s_in.at[0])
    start_in.start()
    tiles_in = pltpu.make_async_copy(tiles_hbm, tiles_ref, s_in.at[1])
    tiles_in.start()

    barrier = pltpu.get_barrier_semaphore()
    for d in range(1, n_row):
        pl.semaphore_signal(
            barrier, inc=1, device_id=(lax.rem(row + d, n_row), col), device_id_type=MESH
        )
    for d in range(1, n_col):
        pl.semaphore_signal(
            barrier, inc=1, device_id=(row, lax.rem(col + d, n_col)), device_id_type=MESH
        )

    def send(src, dst, s_sem, r_sem, target):
        copy = pltpu.make_async_remote_copy(
            src_ref=src,
            dst_ref=dst,
            send_sem=s_sem,
            recv_sem=r_sem,
            device_id=target,
            device_id_type=MESH,
        )
        copy.start()
        return copy

    user_scale = lax.rsqrt(user_degree_ref[pl.ds(col, 1), :].astype(jnp.float32))
    item_scale = lax.rsqrt(item_degree_ref[pl.ds(row, 1), :].astype(jnp.float32))

    def gram_start(raw, way):
        gram = dot_high(raw, raw, NT)
        packed = jnp.concatenate([gram[:half], gram[half:]], axis=1)
        for i in range(n_row):
            gram_own[way, i] = packed[i * part : (i + 1) * part]
        copies = []
        for d in range(1, n_row):
            target = lax.rem(row + d, n_row)
            copies.append(
                send(
                    gram_own.at[way, target],
                    gram_row.at[way, d],
                    s_gr.at[way, d],
                    r_gr.at[way, d],
                    (target, col),
                )
            )
        return copies

    def gram_middle(copies, way):
        total = gram_own[way, row]
        for d in range(1, n_row):
            copies[d - 1].wait_recv()
            total = total + gram_row[way, d]
        gram_sum[way] = total
        out = []
        for d in range(1, n_col):
            out.append(
                send(
                    gram_sum.at[way],
                    gram_col.at[way, d],
                    s_gc.at[way, d],
                    r_gc.at[way, d],
                    (row, lax.rem(col + d, n_col)),
                )
            )
        return out

    def gram_late(copies, way):
        for copy in copies:
            copy.wait_recv()
        gram_col[way, 0] = gram_sum[way]
        total = gram_col[way, col]
        for j in range(1, n_col):
            total = total + gram_col[way, lax.rem(col - j + n_col, n_col)]
        gram_all[way, row] = total
        out = []
        for d in range(1, n_row):
            out.append(
                send(
                    gram_all.at[way, row],
                    gram_all.at[way, row],
                    s_ga.at[way, d],
                    r_ga.at[way, d],
                    (lax.rem(row + d, n_row), col),
                )
            )
        return out

    def gram_end(copies, way):
        for copy in copies:
            copy.wait_recv()
        total = jnp.concatenate([gram_all[way, i] for i in range(n_row)], axis=0)
        gram = jnp.concatenate([total[:, :block], total[:, block:]], axis=0)
        return factor_and_inverse(gram)

    def put_split(h, first_block, values):
        for b in range(values.shape[1] // width):
            piece = values[:, b * width : (b + 1) * width]
            high = piece.astype(jnp.bfloat16)
            low = (piece - high.astype(jnp.float32)).astype(jnp.bfloat16)
            split[h, first_block + b] = jnp.concatenate([high, low], axis=0)

    def products(h, base, dims):
        def one(t, total):
            tile = tiles_ref[index_ref[base + t]]
            vectors = split[h, index_ref[base + slots + t]]
            keep = index_ref[base + 2 * slots + t].astype(jnp.float32)
            both = lax.dot_general(
                vectors, tile, dims, preferred_element_type=jnp.float32
            )
            total = total * keep + (both[:half] + both[half:])
            running[h, t] = total
            return total

        lax.fori_loop(0, slots, one, jnp.zeros((half, width), jnp.float32), unroll=16)

    forward_base = 0
    forward_last = 3 * slots
    backward_base = forward_last + row_blocks
    backward_last = backward_base + 3 * slots

    for h in range(2):
        running[h, slots] = jnp.zeros((half, width), jnp.float32)
    user_basis[...] = jnp.zeros_like(user_basis)
    start_in.wait()
    pl.semaphore_wait(barrier, n_row + n_col - 2)
    tiles_in.wait()

    def step(k, carry):
        raw = item_raw[...]
        scaled = raw * item_scale
        moved = [[], []]

        def send_items(h):
            item_all[h, row] = scaled[h * half : (h + 1) * half]
            for d in range(1, n_row):
                moved[h].append(
                    send(
                        item_all.at[h, row],
                        item_all.at[h, row],
                        s_ir.at[h, d],
                        r_ir.at[h, d],
                        (lax.rem(row + d, n_row), col),
                    )
                )

        def take_items(h):
            for d in range(1, n_row):
                moved[h][d - 1].wait_recv()
                source = lax.rem(row - d + n_row, n_row)
                put_split(h, source * item_per, item_all[h, source])

        pair = [[], []]
        across = [[], []]

        def send_pair(h):
            for core_at in range(2):
                for z_at in range(n_z):
                    for b in range(user_per):
                        owned = (z_at * 2 + core_at) * user_per + b
                        user_send[
                            h, core_at * n_z + z_at, :, b * width : (b + 1) * width
                        ] = running[h, index_ref[forward_last + owned]]
            pair[h].append(
                send(
                    user_send.at[h, pl.ds((1 - core) * n_z, n_z)],
                    sibling_in.at[h],
                    s_sib.at[h],
                    r_sib.at[h],
                    (row, sibling),
                )
            )

        def send_across(h):
            pair[h][0].wait_recv()
            for d in range(1, n_z):
                target_z = lax.rem(z + d, n_z)
                user_send2[h, target_z] = (
                    user_send[h, core * n_z + target_z] + sibling_in[h, target_z]
                )
                across[h].append(
                    send(
                        user_send2.at[h, target_z],
                        user_in.at[h, z],
                        s_z.at[h, d],
                        r_z.at[h, d],
                        (row, target_z * 2 + core),
                    )
                )
            return user_send[h, core * n_z + z] + sibling_in[h, z]

        send_items(0)
        sent = gram_start(raw, 0)
        send_items(1)
        for h in range(2):
            put_split(h, row * item_per, scaled[h * half : (h + 1) * half])
        take_items(0)
        sent2 = gram_middle(sent, 0)
        products(0, forward_base, NT)
        send_pair(0)
        take_items(1)
        summed0 = send_across(0)
        products(1, forward_base, NT)
        send_pair(1)
        sent3 = gram_late(sent2, 0)
        summed1 = send_across(1)
        factor_t, inverse = gram_end(sent3, 0)
        right_factor_ref[lax.rem(k + STEPS - 1, STEPS)] = factor_t.T
        item_basis[...] = dot_high(inverse, raw)
        correction = dot_high(factor_t, user_basis[...])
        for group in [sent, sent2, sent3] + moved + pair:
            for copy in group:
                copy.wait_send()
        sums = [summed0, summed1]
        for h in range(2):
            for d in range(1, n_z):
                across[h][d - 1].wait_recv()
                sums[h] = sums[h] + user_in[h, lax.rem(z - d + n_z, n_z)]
        summed = jnp.concatenate(sums, axis=0)
        forward = dot_high(inverse, summed * user_scale) - correction

        scaled = forward * user_scale
        moved_u = [[], []]
        passed = [[], []]

        def send_users(h):
            user_all[h, col] = scaled[h * half : (h + 1) * half]
            for d in range(1, n_z):
                moved_u[h].append(
                    send(
                        user_all.at[h, col],
                        user_all.at[h, col],
                        s_uz.at[h, d],
                        r_uz.at[h, d],
                        (row, lax.rem(z + d, n_z) * 2 + core),
                    )
                )
            pass_on(h, col, 0)

        def pass_on(h, source, d):
            passed[h].append(
                send(
                    user_all.at[h, source],
                    user_all.at[h, source],
                    s_us.at[h, d],
                    r_us.at[h, d],
                    (row, sibling),
                )
            )

        def take_users(h):
            passed[h][0].wait_recv()
            put_split(h, sibling * user_per, user_all[h, sibling])
            for d in range(1, n_z):
                moved_u[h][d - 1].wait_recv()
                source = lax.rem(z - d + n_z, n_z) * 2 + core
                pass_on(h, source, d)
                put_split(h, source * user_per, user_all[h, source])
            for d in range(1, n_z):
                passed[h][d].wait_recv()
                source = lax.rem(z - d + n_z, n_z) * 2 + 1 - core
                put_split(h, source * user_per, user_all[h, source])

        back = [[], []]

        def send_rows(h):
            for j in range(n_row):
                for b in range(item_per):
                    item_send[h, j, :, b * width : (b + 1) * width] = running[
                        h, index_ref[backward_last + j * item_per + b]
                    ]
            for d in range(1, n_row):
                target = lax.rem(row + d, n_row)
                back[h].append(
                    send(
                        item_send.at[h, target],
                        item_in.at[h, row],
                        s_row.at[h, d],
                        r_row.at[h, d],
                        (target, col),
                    )
                )

        send_users(0)
        sent = gram_start(forward, 1)
        send_users(1)
        for copy in across[0] + across[1]:
            copy.wait_send()
        for h in range(2):
            put_split(h, col * user_per, scaled[h * half : (h + 1) * half])
        sent2 = gram_middle(sent, 1)
        take_users(0)
        products(0, backward_base, NN)
        send_rows(0)
        sent3 = gram_late(sent2, 1)
        take_users(1)
        products(1, backward_base, NN)
        send_rows(1)
        factor_t, inverse = gram_end(sent3, 1)
        left_factor_ref[k] = factor_t.T
        user_basis[...] = dot_high(inverse, forward)
        correction = dot_high(factor_t, item_basis[...])
        for group in [sent, sent2, sent3] + moved_u + passed:
            for copy in group:
                copy.wait_send()
        sums = []
        for h in range(2):
            total = item_send[h, row]
            for d in range(1, n_row):
                back[h][d - 1].wait_recv()
                total = total + item_in[h, lax.rem(row - d + n_row, n_row)]
            sums.append(total)
        summed = jnp.concatenate(sums, axis=0)
        item_raw[...] = dot_high(inverse, summed * item_scale) - correction
        for copy in back[0] + back[1]:
            copy.wait_send()
        return carry

    lax.fori_loop(0, STEPS, step, 0)

    raw = item_raw[...]
    sent = gram_start(raw, 0)
    left_ref[...] = user_basis[...] * math.sqrt(row_blocks * width * n_row)
    sent2 = gram_middle(sent, 0)
    sent3 = gram_late(sent2, 0)
    factor_t, inverse = gram_end(sent3, 0)
    right_factor_ref[STEPS - 1] = factor_t.T
    right_ref[...] = dot_high(inverse, raw) * math.sqrt(col_blocks * width * n_col)
    for copy in sent + sent2 + sent3:
        copy.wait_send()


def order_tables(keys, partners, live, blocks):
    slots = keys.shape[0]
    at = jnp.arange(slots)
    rank_key = jnp.where(live, keys, blocks) * slots + at
    rank = jnp.sum((rank_key[None, :] < rank_key[:, None]).astype(jnp.int32), axis=1)
    placed = rank[None, :] == at[:, None]
    order = jnp.sum(jnp.where(placed, at[None, :], 0), axis=1)
    partner = jnp.sum(jnp.where(placed, partners[None, :], 0), axis=1)
    same = (keys[None, :] == keys[:, None]) & (live[None, :] & live[:, None])
    earlier = jnp.any(same & (at[None, :] < at[:, None]), axis=1)
    keep = jnp.sum(jnp.where(placed, earlier[None, :].astype(jnp.int32), 0), axis=1)
    mine = (keys[None, :] == jnp.arange(blocks)[:, None]) & live[None, :]
    last = jnp.max(jnp.where(mine, rank[None, :], -1), axis=1)
    last = jnp.where(last < 0, slots, last)
    return [order, partner, keep, last]


def per_device(tiles, tile_slots, tile_counts, user_degree, item_degree, start_panel):
    n_row, n_col = lax.axis_size("row"), lax.axis_size("col")
    slots, width = tiles.shape[2], tiles.shape[3]
    block = start_panel.shape[0]
    row_blocks = user_degree.shape[0] // width
    col_blocks = item_degree.shape[0] // width
    user_group = user_degree.shape[0] // n_col
    item_group = item_degree.shape[0] // n_row
    slot_list = tile_slots[0, 0]
    live = jnp.arange(slots) < tile_counts[0, 0]
    slot_list = jnp.where(live, slot_list, 0)
    local_rows, local_cols = slot_list // col_blocks, slot_list % col_blocks
    index = jnp.concatenate(
        order_tables(local_rows, local_cols, live, row_blocks)
        + order_tables(local_cols, local_rows, live, col_blocks)
    ).astype(jnp.int32)
    vmem = pl.BlockSpec(memory_space=pltpu.VMEM)
    f32 = jnp.float32
    dma = pltpu.SemaphoreType.DMA
    n_z = n_col // 2
    half = block // 2
    part = half // n_row
    anywhere = pl.BlockSpec(memory_space=pl.ANY)
    out = pl.pallas_call(
        functools.partial(kernel, n_row, n_col, row_blocks, col_blocks),
        out_shape=(
            jax.ShapeDtypeStruct((block, user_group), f32),
            jax.ShapeDtypeStruct((block, item_group), f32),
            jax.ShapeDtypeStruct((STEPS, block, block), f32),
            jax.ShapeDtypeStruct((STEPS, block, block), f32),
        ),
        in_specs=[pl.BlockSpec(memory_space=pltpu.SMEM), anywhere, vmem, vmem, anywhere],
        out_specs=(vmem,) * 4,
        scratch_shapes=[
            pltpu.VMEM((slots, width, width), tiles.dtype),
            pltpu.VMEM((2, n_row, half, item_group), f32),
            pltpu.VMEM((2, n_col, half, user_group), f32),
            pltpu.VMEM((2, max(row_blocks, col_blocks), block, width), jnp.bfloat16),
            pltpu.VMEM((2, slots + 1, half, width), f32),
            pltpu.VMEM((2, n_col, half, user_group), f32),
            pltpu.VMEM((2, n_z, half, user_group), f32),
            pltpu.VMEM((2, n_z, half, user_group), f32),
            pltpu.VMEM((2, n_z, half, user_group), f32),
            pltpu.VMEM((2, n_row, half, item_group), f32),
            pltpu.VMEM((2, n_row, half, item_group), f32),
            pltpu.VMEM((block, item_group), f32),
            pltpu.VMEM((block, item_group), f32),
            pltpu.VMEM((block, user_group), f32),
            pltpu.VMEM((2, n_row, part, 2 * block), f32),
            pltpu.VMEM((2, n_row, part, 2 * block), f32),
            pltpu.VMEM((2, part, 2 * block), f32),
            pltpu.VMEM((2, n_col, part, 2 * block), f32),
            pltpu.VMEM((2, n_row, part, 2 * block), f32),
            dma((2,)),
            dma((2, n_row)),
            dma((2, n_row)),
            dma((2, n_col)),
            dma((2, n_col)),
            dma((2, n_row)),
            dma((2, n_row)),
            dma((2, n_row)),
            dma((2, n_row)),
            dma((2, n_z)),
            dma((2, n_z)),
            dma((2, n_z)),
            dma((2, n_z)),
            dma((2,)),
            dma((2,)),
            dma((2, n_z)),
            dma((2, n_z)),
            dma((2, n_row)),
            dma((2, n_row)),
        ],
        compiler_params=pltpu.CompilerParams(
            collective_id=0, has_side_effects=True, vmem_limit_bytes=63 * 1024 * 1024
        ),
    )(
        index,
        tiles[0, 0],
        user_degree.reshape(n_col, user_group),
        item_degree.reshape(n_row, item_group),
        start_panel,
    )
    return tuple(out)


def solution(mesh):
    in_specs = (
        P("row", "col", None, None, None),
        P("row", "col", None),
        P("row", "col"),
        P("row"),
        P("col"),
        P(None, ("col", "row")),
    )
    out_specs = (P(None, ("row", "col")), P(None, ("col", "row")), P(), P())
    def whole(*args):
        tile_width = args[0].shape[3]
        cells = mesh.shape["row"] * mesh.shape["col"]
        owned = (args[3].shape[0] // cells, args[4].shape[0] // cells)
        form = per_device
        sliver = (args[5].shape[0] // 2) % (8 * mesh.shape["row"])
        if owned[0] % tile_width or owned[1] % tile_width or sliver:
            form = per_device_arrays
        return jax.shard_map(
            form, mesh=mesh, in_specs=in_specs, out_specs=out_specs, check_vma=False
        )(*args)

    return whole
```
